128 devices in a mesh: row: 16 (over x, z), col: 8 (over y, core).
Axes of the slice: x: 4, y: 4, z: 4, core: 2. Of those that a mesh axis runs over, the one named last changes fastest.
Arguments:
- momentum: float32 [28672, 8192], P('row', 'col'), may hold values from -6 to 6
- gradient: bfloat16 [28672, 8192], P('row', 'col'), may hold values from -180 to 180, as said below
- right_factor: bfloat16 [8192, 512], P('col'), may hold values from -6 to 6
Outputs:
- left_factor: float32 [28672, 512], P('row')
- momentum_next: float32 [28672, 8192], P('row', 'col')
- right_next: bfloat16 [8192, 512], P('col')
The draws below stay inside these ranges and needn't reach their ends.
Inputs may be any that keep to these rules, and one draw needn't show every extreme that they name: gradient of the layer.
All inputs are finite; a program needn't handle non-finite values.
Results may differ from the reference program's by a relative error of at most 0.0046.
Values sent between devices are 32-bit elements; how exact they have to be, the bound alone decides.
No kernel may reach another device: no remote copies, remote signals or barrier semaphores. Data moves between devices by JAX's collectives and lax.ppermute only.
A program may use at most 128 MiB of HBM per device.

```python
import math
import jax
import jax.numpy as jnp
from jax import lax

FF = 28672
D = 8192
RANK = 512


def draw_gradient(key, part):
    key = jax.random.fold_in(key, 7)
    key_rows, key_cols, key_base = jax.random.split(key, 3)
    row_pos = jnp.arange(FF, dtype=jnp.float32) / FF
    col_pos = jnp.arange(D, dtype=jnp.float32) / D
    row_scale = (1.0 + 2.0 * row_pos) * jnp.exp(jax.random.uniform(key_rows, (FF,), jnp.float32, 0.0, math.log(10.0)))
    col_scale = (1.0 + 2.0 * col_pos) * jnp.exp(jax.random.uniform(key_cols, (D,), jnp.float32, 0.0, math.log(10.0)))
    base = jnp.clip(jax.random.normal(key_base, (FF, D), jnp.float32), -4.0, 4.0)
    values = 0.05 * base * row_scale[:, None] * col_scale[None, :]
    return values.astype(jnp.bfloat16)


def block_scale(rng, extent, cuts, low, largest):
    factor_of, own = 1.0, jax.random.fold_in(rng, 6)
    for axis_at, blocks in cuts:
        heights = jnp.exp(jax.random.uniform(jax.random.fold_in(own, axis_at), (blocks,), jnp.float32, low / len(cuts), largest / len(cuts)))
        factor_of = factor_of * jnp.repeat(heights, extent[axis_at] // blocks).reshape([-1 if axis == axis_at else 1 for axis in range(len(extent))])
    return factor_of


def scatter_about(own_key, extent, spread, most, cuts=(), held_as=jnp.bfloat16):
    loudness = block_scale(own_key, extent, cuts, -0.22, 0.18) if cuts else 1.0
    array = jax.random.normal(own_key, extent, jnp.float32) * spread * loudness
    return jnp.minimum(jnp.maximum(array, -most), most).astype(held_as)


def setup_inputs(seed: int = 0) -> dict:
    arg_keys = jax.random.split(jax.random.key(seed), 4)
    momentum = scatter_about(arg_keys[0], (FF, D), 1.0, 6.0, ((0, 16), (1, 8)), jnp.float32)
    gradient = draw_gradient(jax.random.fold_in(arg_keys[3], 71), 0)
    right_factor = scatter_about(arg_keys[2], (D, RANK), 1.0, 6.0, ((0, 8),))
    return dict(momentum=momentum, gradient=gradient, right_factor=right_factor)


def reference(momentum, gradient, right_factor):
    count = 16
    height = FF // count
    mom_blocks = momentum.reshape(count, height, D)
    grad_blocks = gradient.reshape(count, height, D)

    def power_block(pair):
        summed = pair[0] + pair[1].astype(jnp.float32)
        return jnp.dot(summed.astype(jnp.bfloat16).astype(jnp.float32), right_factor.astype(jnp.float32), preferred_element_type=jnp.float32)
    power = lax.map(power_block, (mom_blocks, grad_blocks)).reshape(FF, RANK)
    gram = jnp.dot(power.T.astype(jnp.float32), power.astype(jnp.float32), precision=lax.Precision.HIGHEST, preferred_element_type=jnp.float32)
    lower = jnp.linalg.cholesky(gram)
    ortho = jax.scipy.linalg.solve_triangular(lower, power.T, lower=True).T
    left_factor = ortho * jnp.sqrt(jnp.float32(FF))
    left_low = ortho.astype(jnp.bfloat16)
    left_blocks = left_low.reshape(count, height, RANK)

    def cross_step(total, items):
        summed = items[0] + items[1].astype(jnp.float32)
        part = lax.dot_general(summed.astype(jnp.bfloat16).astype(jnp.float32), items[2].astype(jnp.float32), (((0,), (0,)), ((), ())), preferred_element_type=jnp.float32)
        return (total + part, None)
    cross, unused = lax.scan(cross_step, jnp.zeros((D, RANK), jnp.float32), (mom_blocks, grad_blocks, left_blocks))
    cross_low = cross.astype(jnp.bfloat16)

    def update_block(items):
        summed = items[0] + items[1].astype(jnp.float32)
        return summed - 0.05 * lax.dot_general(items[2].astype(jnp.float32), cross_low.astype(jnp.float32), (((1,), (1,)), ((), ())), preferred_element_type=jnp.float32)
    momentum_next = lax.map(update_block, (mom_blocks, grad_blocks, left_blocks)).reshape(FF, D)
    colsq = lax.optimization_barrier(jnp.sum(cross * cross, axis=0))
    right_next = (cross / jnp.sqrt(colsq / D + 1e-06)).astype(jnp.bfloat16)
    return (left_factor, momentum_next, right_next)
```

```python
import functools

import jax
import jax.numpy as jnp
from jax import lax
from jax.experimental import pallas as pl
from jax.experimental.pallas import tpu as pltpu
from jax.sharding import PartitionSpec as P

FF = 28672
D = 8192
RANK = 512
ROWS = 1792
COLS = 1024
CHUNK = 224
BLOCK = 128
AXES = ("row", "col")
HIGHEST = lax.Precision.HIGHEST
MIB = 2**20
F32 = jnp.float32
BF16 = jnp.bfloat16


def place(x, z, y, core):
    return (x * 4 + z) * 8 + y * 2 + core


def pairs_of(move):
    out = []
    for x in range(4):
        for z in range(4):
            for y in range(4):
                for core in range(2):
                    out.append((place(x, z, y, core), place(*move(x, z, y, core))))
    return out


def to_partner(value):
    return lax.ppermute(value, AXES, pairs_of(lambda x, z, y, core: (x, z, y, 1 - core)))


def along_y(value, step):
    return lax.ppermute(value, AXES, pairs_of(lambda x, z, y, core: (x, z, (y + step) % 4, core)))


def along_first(value, step):
    def move(x, z, y, core):
        return ((x + step) % 4, z, y, core) if core == 0 else (x, (z + step) % 4, y, core)

    return lax.ppermute(value, AXES, pairs_of(move))


def along_second(value, step):
    def move(x, z, y, core):
        return (x, (z + step) % 4, y, core) if core == 0 else ((x + step) % 4, z, y, core)

    return lax.ppermute(value, AXES, pairs_of(move))


def scattered_sum(blocks, mine, along):
    def block(step):
        return lax.dynamic_index_in_dim(blocks, (mine + step) % 4, 0, keepdims=False)

    got = [along(block(step), step) for step in (2, 1, 3)]
    return (block(0) + got[0]) + (got[1] + got[2])


def exchanged_sum(value, along):
    got = [along(value, step) for step in (2, 1, 3)]
    return (value + got[0]) + (got[1] + got[2])


def gathered(value, along):
    got = {step: along(value, -step) for step in (2, 1, 3)}
    return [value, got[1], got[2], got[3]]


def dot(a, b, precision=None):
    return lax.dot_general(
        a, b, (((1,), (0,)), ((), ())), precision=precision, preferred_element_type=F32
    )


def dot_t(a, b, precision=None):
    return lax.dot_general(
        a, b, (((0,), (0,)), ((), ())), precision=precision, preferred_element_type=F32
    )


def halves(value):
    high = value.astype(BF16)
    return high, (value - high.astype(F32)).astype(BF16)


def dot3(a, b):
    ah, al = halves(a)
    bh, bl = halves(b)
    return dot(ah, bh) + (dot(ah, bl) + dot(al, bh))


def params(mib):
    return pltpu.CompilerParams(vmem_limit_bytes=mib * MIB)


def whole(shape):
    return pl.BlockSpec(shape, lambda *_: (0,) * len(shape))


def power_kernel(where, momentum, gradient, right, power, lowered):
    low = (momentum[...] + gradient[...].astype(F32)).astype(BF16)
    lowered[0] = low
    power[0] = dot(low, right[...])


def power_part(momentum, gradient, right, core):
    rows = lambda i, where: (2 * i + where[0], 0)
    return pl.pallas_call(
        power_kernel,
        grid_spec=pltpu.PrefetchScalarGridSpec(
            num_scalar_prefetch=1,
            grid=(4,),
            in_specs=[
                pl.BlockSpec((CHUNK, COLS), rows),
                pl.BlockSpec((CHUNK, COLS), rows),
                whole((COLS, RANK)),
            ],
            out_specs=[
                pl.BlockSpec((1, CHUNK, RANK), lambda i, where: (i, 0, 0)),
                pl.BlockSpec((1, CHUNK, COLS), lambda i, where: (i, 0, 0)),
            ],
        ),
        out_shape=[
            jax.ShapeDtypeStruct((4, CHUNK, RANK), F32),
            jax.ShapeDtypeStruct((4, CHUNK, COLS), BF16),
        ],
        compiler_params=params(24),
        cost_estimate=pl.CostEstimate(
            flops=ROWS * COLS * RANK, bytes_accessed=10 * MIB, transcendentals=0
        ),
        name="power_part",
    )(core.reshape(1), momentum, gradient, right)


def gram_kernel(where, own, other, out):
    def strip(lo, hi, at):
        total = dot_t(own[:, lo:hi], own[:, at : at + BLOCK], HIGHEST)
        return total + dot_t(other[:, lo:hi], other[:, at : at + BLOCK], HIGHEST)

    @pl.when(where[0] == 0)
    def _():
        out[0:128] = strip(0, 128, 0)
        out[128:640] = strip(0, 512, 384)

    @pl.when(where[0] == 1)
    def _():
        out[0:256] = strip(0, 256, 128)
        out[256:640] = strip(0, 384, 256)


def gram_part(core, own, other):
    return pl.pallas_call(
        gram_kernel,
        grid_spec=pltpu.PrefetchScalarGridSpec(
            num_scalar_prefetch=1,
            grid=(1,),
            in_specs=[whole((CHUNK, RANK))] * 2,
            out_specs=whole((640, BLOCK)),
        ),
        out_shape=jax.ShapeDtypeStruct((640, BLOCK), F32),
        compiler_params=params(16),
        cost_estimate=pl.CostEstimate(flops=10**9, bytes_accessed=2 * MIB, transcendentals=0),
        name="gram_part",
    )(core.reshape(1), own, other)


def block_inverse(matrix, eye):
    rows = lax.broadcasted_iota(jnp.int32, (8, BLOCK), 0)
    tile = (8, BLOCK)
    A = [matrix[8 * g : 8 * g + 8, :] for g in range(16)]
    E = [eye[8 * g : 8 * g + 8, :] for g in range(16)]
    out = []
    for p in range(16):
        col = {}
        for g in range(p, 16):
            for k in range(8):
                col[g, k] = jnp.broadcast_to(A[g][:, 8 * p + k : 8 * p + k + 1], tile)
        one = {}
        for k in range(8):
            for l in range(k, 8):
                one[k, l] = jnp.broadcast_to(col[p, k][l : l + 1, :], tile)
        row_a = [jnp.broadcast_to(A[p][k : k + 1, :], tile) for k in range(8)]
        row_e = [jnp.broadcast_to(E[p][k : k + 1, :], tile) for k in range(8)]
        done = []
        for k in range(8):
            inv = 1.0 / one[k, k]
            mult = {l: one[k, l] * inv for l in range(k + 1, 8)}
            for i in range(k + 1, 8):
                for l in range(i, 8):
                    one[i, l] = one[i, l] - one[k, i] * mult[l]
            scaled_a = row_a[k] * inv
            scaled_e = row_e[k] * inv
            for l in range(k + 1, 8):
                row_a[l] = row_a[l] - row_a[k] * mult[l]
                row_e[l] = row_e[l] - row_e[k] * mult[l]
            for g in range(p + 1, 16):
                for l in range(k + 1, 8):
                    col[g, l] = col[g, l] - col[g, k] * mult[l]
                A[g] = A[g] - col[g, k] * scaled_a
                E[g] = E[g] - col[g, k] * scaled_e
            done.append(row_e[k] * lax.rsqrt(one[k, k]))
        tile_out = done[0]
        for k in range(1, 8):
            tile_out = jnp.where(rows == k, done[k], tile_out)
        out.append(tile_out)
    return jnp.concatenate(out, axis=0)


def inverse_kernel(where, mine, theirs, x_ref, xt_ref, strips, a, e):
    core = where[0]
    for slot, source, first in ((core, mine, where[1]), (1 - core, theirs, where[2])):
        for step in range(4):
            at = pl.multiple_of(lax.rem(first + step, 4) * 160, 32)
            strips[slot, pl.ds(at, 160), :] = source[160 * step : 160 * step + 160, :]
    a[0:128, 0:128] = strips[0, 0:128]
    a[0:512, 384:512] = strips[0, 128:640]
    a[0:256, 128:256] = strips[1, 0:256]
    a[0:384, 256:384] = strips[1, 256:640]
    eye = (
        lax.broadcasted_iota(jnp.int32, (BLOCK, BLOCK), 0)
        == lax.broadcasted_iota(jnp.int32, (BLOCK, BLOCK), 1)
    ).astype(F32)
    x_ref[...] = jnp.zeros_like(x_ref)
    e[...] = jnp.zeros_like(e)
    for lo in range(0, RANK, BLOCK):
        hi = lo + BLOCK
        inverse = block_inverse(a[lo:hi, lo:hi], eye)
        x_ref[lo:hi, lo:hi] = inverse
        if lo > 0:
            x_ref[lo:hi, :lo] = dot(inverse, e[lo:hi, :lo], HIGHEST)
        if hi < RANK:
            upper = dot(inverse, a[lo:hi, hi:], HIGHEST)
            a[hi:, hi:] = a[hi:, hi:] - dot_t(upper, upper, HIGHEST)
            e[hi:, :hi] = e[hi:, :hi] - dot_t(upper, x_ref[lo:hi, :hi], HIGHEST)
    xt_ref[...] = x_ref[...].T


def inverse_factor(where, mine, theirs):
    return pl.pallas_call(
        inverse_kernel,
        grid_spec=pltpu.PrefetchScalarGridSpec(
            num_scalar_prefetch=1,
            grid=(1,),
            in_specs=[whole((640, BLOCK))] * 2,
            out_specs=[whole((RANK, RANK))] * 2,
            scratch_shapes=[
                pltpu.VMEM((2, 640, BLOCK), F32),
                pltpu.VMEM((RANK, RANK), F32),
                pltpu.VMEM((RANK, RANK), F32),
            ],
        ),
        out_shape=[jax.ShapeDtypeStruct((RANK, RANK), F32)] * 2,
        compiler_params=params(24),
        cost_estimate=pl.CostEstimate(
            flops=2 * 10**10, bytes_accessed=4 * MIB, transcendentals=0
        ),
        name="inverse_factor",
    )(where, mine, theirs)


def product_kernel(where, *refs):
    own, other = refs[0:4], refs[4:8]
    low_own, low_other, out, power, high, low = refs[8:]
    core, y = where[0], where[3]

    @pl.when(pl.program_id(0) == 0)
    def _():
        for side, source in ((0, own), (1, other)):
            chunk_core = core if side == 0 else 1 - core
            for step in range(4):
                at = lax.rem(y + step, 4)
                value = source[step][...]
                power[2 * at + chunk_core] = value
                first, second = halves(value)
                rows = pl.ds(pl.multiple_of(at * CHUNK, CHUNK), CHUNK)
                high[side, rows, :] = first
                low[side, rows, :] = second

    a = low_own[...].reshape(4 * CHUNK, -1)
    b = low_other[...].reshape(4 * CHUNK, -1)
    total = dot_t(low[0], a) + dot_t(low[1], b)
    out[...] = total + (dot_t(high[0], a) + dot_t(high[1], b))


def product(where, own, other, low_own, low_other):
    width = 256
    low_spec = pl.BlockSpec((4, CHUNK, width), lambda j, where: (0, 0, j))
    return pl.pallas_call(
        product_kernel,
        grid_spec=pltpu.PrefetchScalarGridSpec(
            num_scalar_prefetch=1,
            grid=(COLS // width,),
            in_specs=[whole((CHUNK, RANK))] * 8 + [low_spec] * 2,
            out_specs=[
                pl.BlockSpec((RANK, width), lambda j, where: (0, j)),
                whole((8, CHUNK, RANK)),
            ],
            scratch_shapes=[
                pltpu.VMEM((2, 4 * CHUNK, RANK), BF16),
                pltpu.VMEM((2, 4 * CHUNK, RANK), BF16),
            ],
        ),
        out_shape=[
            jax.ShapeDtypeStruct((RANK, COLS), F32),
            jax.ShapeDtypeStruct((8, CHUNK, RANK), F32),
        ],
        compiler_params=params(40),
        cost_estimate=pl.CostEstimate(
            flops=4 * ROWS * COLS * RANK, bytes_accessed=12 * MIB, transcendentals=0
        ),
        name="product",
    )(where, *own, *other, low_own, low_other)


def cross_kernel(where, p0, p1, p2, p3, x_ref, cross_low, cross, colsq, total):
    first = where[1]
    for step, piece in enumerate((p0, p1, p2, p3)):
        at = pl.multiple_of(lax.rem(first + step, 4) * BLOCK, BLOCK)
        total[pl.ds(at, BLOCK), :] = piece[...]
    value = dot3(x_ref[...], total[...])
    cross_low[...] = value.astype(BF16)
    turned = value.T
    cross[...] = turned
    colsq[...] = jnp.sum((turned * turned).reshape(COLS // 8, 8, RANK), axis=0)


def cross_of(where, pieces, x):
    return pl.pallas_call(
        cross_kernel,
        grid_spec=pltpu.PrefetchScalarGridSpec(
            num_scalar_prefetch=1,
            grid=(1,),
            in_specs=[whole((BLOCK, COLS))] * 4 + [whole((RANK, RANK))],
            out_specs=[whole((RANK, COLS)), whole((COLS, RANK)), whole((8, RANK))],
            scratch_shapes=[pltpu.VMEM((RANK, COLS), F32)],
        ),
        out_shape=[
            jax.ShapeDtypeStruct((RANK, COLS), BF16),
            jax.ShapeDtypeStruct((COLS, RANK), F32),
            jax.ShapeDtypeStruct((8, RANK), F32),
        ],
        compiler_params=params(40),
        cost_estimate=pl.CostEstimate(
            flops=6 * COLS * RANK * RANK, bytes_accessed=6 * MIB, transcendentals=0
        ),
        name="cross_of",
    )(where, *pieces, x)


def update_kernel(momentum, gradient, power, xt, cross_low, left, momentum_next):
    ortho = dot3(power[0], xt[...])
    left[...] = ortho * jnp.sqrt(F32(FF))
    feedback = dot(ortho.astype(BF16), cross_low[...])
    summed = momentum[...] + gradient[...].astype(F32)
    momentum_next[...] = summed - 0.05 * feedback


def update(momentum, gradient, power, xt, cross_low):
    rows = lambda i: (i, 0)
    return pl.pallas_call(
        update_kernel,
        grid=(8,),
        in_specs=[
            pl.BlockSpec((CHUNK, COLS), rows),
            pl.BlockSpec((CHUNK, COLS), rows),
            pl.BlockSpec((1, CHUNK, RANK), lambda i: (i, 0, 0)),
            whole((RANK, RANK)),
            whole((RANK, COLS)),
        ],
        out_specs=[pl.BlockSpec((CHUNK, RANK), rows), pl.BlockSpec((CHUNK, COLS), rows)],
        out_shape=[
            jax.ShapeDtypeStruct((ROWS, RANK), F32),
            jax.ShapeDtypeStruct((ROWS, COLS), F32),
        ],
        compiler_params=params(32),
        cost_estimate=pl.CostEstimate(
            flops=6 * ROWS * RANK * RANK, bytes_accessed=26 * MIB, transcendentals=0
        ),
        name="update",
    )(momentum, gradient, power, xt, cross_low)


def on_device(momentum, gradient, right_factor):
    row = lax.axis_index("row")
    col = lax.axis_index("col")
    x, z, y, core = row // 4, row % 4, col // 2, col % 2
    first = jnp.where(core == 0, x, z)
    second = jnp.where(core == 0, z, x)
    where = jnp.stack([core, first, second, y]).astype(jnp.int32)

    theirs, low_other = power_part(momentum, gradient, right_factor, 1 - core)
    got = to_partner(theirs)
    mine, low_own = power_part(momentum, gradient, right_factor, core)
    own = scattered_sum(mine + got, y, along_y)
    other = to_partner(own)

    gram = gram_part(core, own, other).reshape(4, 160, BLOCK)
    gram = scattered_sum(gram, first, along_first)
    gram = exchanged_sum(gram, along_second)
    gram = exchanged_sum(gram, along_y)
    gram = jnp.concatenate(gathered(gram, along_first), axis=0)
    inverse, inverse_t = inverse_factor(where, gram, to_partner(gram))

    own_all = gathered(own, along_y)
    others = to_partner(jnp.concatenate(own_all[1:], axis=0))
    other_all = [other] + [others[CHUNK * i : CHUNK * (i + 1)] for i in range(3)]
    turned, power = product(where, own_all, other_all, low_own, low_other)
    turned = scattered_sum(turned.reshape(4, BLOCK, COLS), first, along_first)
    turned = scattered_sum(turned.reshape(4, 32, COLS), second, along_second)
    turned = gathered(turned, along_second)
    turned = jnp.roll(jnp.stack(turned), second, axis=0).reshape(BLOCK, COLS)
    pieces = gathered(turned, along_first)

    cross_low, cross, colsq = cross_of(where, pieces, inverse)
    colsq = jnp.sum(colsq, axis=0, keepdims=True)
    colsq = exchanged_sum(colsq, along_y)
    colsq = colsq + to_partner(colsq)
    left_factor, momentum_next = update(momentum, gradient, power, inverse_t, cross_low)
    right_next = (cross / jnp.sqrt(colsq / D + 1e-06)).astype(BF16)
    return (left_factor, momentum_next, right_next)


def solution(mesh):
    in_specs = (P("row", "col"), P("row", "col"), P("col", None))
    out_specs = (P("row", None), P("row", "col"), P("col", None))
    return jax.shard_map(
        on_device, mesh=mesh, in_specs=in_specs, out_specs=out_specs, check_vma=False
    )
```

```python
import functools

import jax
import jax.numpy as jnp
from jax import lax
from jax.experimental import pallas as pl
from jax.experimental.pallas import tpu as pltpu
from jax.sharding import PartitionSpec as P

FF = 28672
D = 8192
RANK = 512
ROWS = 1792
COLS = 1024
CHUNK = 224
PAIR = 448
ORDER = (2, 1, 3, 0)
BLOCK = 128
AXES = ("row", "col")
HIGHEST = lax.Precision.HIGHEST
MIB = 2**20
F32 = jnp.float32
BF16 = jnp.bfloat16


def place(x, z, y, core):
    return (x * 4 + z) * 8 + y * 2 + core


def pairs_of(move):
    out = []
    for x in range(4):
        for z in range(4):
            for y in range(4):
                for core in range(2):
                    out.append((place(x, z, y, core), place(*move(x, z, y, core))))
    return out


def to_partner(value):
    return lax.ppermute(value, AXES, pairs_of(lambda x, z, y, core: (x, z, y, 1 - core)))


def along_y(value, step):
    return lax.ppermute(value, AXES, pairs_of(lambda x, z, y, core: (x, z, (y + step) % 4, core)))


def along_first(value, step):
    def move(x, z, y, core):
        return ((x + step) % 4, z, y, core) if core == 0 else (x, (z + step) % 4, y, core)

    return lax.ppermute(value, AXES, pairs_of(move))


def along_second(value, step):
    def move(x, z, y, core):
        return (x, (z + step) % 4, y, core) if core == 0 else ((x + step) % 4, z, y, core)

    return lax.ppermute(value, AXES, pairs_of(move))


def tied(value, after):
    return value if after is None else lax.optimization_barrier((value, after))[0]


def total_of(own, got, after):
    got = [tied(part, after) for part in got]
    return (own + got[0]) + (got[1] + got[2])


def scattered_sum(blocks, along, after=None):
    return total_of(blocks[0], [along(blocks[step], step) for step in (2, 1, 3)], after)


def exchanged_sum(value, along, after=None):
    return total_of(value, [along(value, step) for step in (2, 1, 3)], after)


def gathered(value, along):
    got = {step: along(value, -step) for step in (2, 1, 3)}
    return [value, got[1], got[2], got[3]]


def dot(a, b, precision=None):
    return lax.dot_general(
        a, b, (((1,), (0,)), ((), ())), precision=precision, preferred_element_type=F32
    )


def dot_t(a, b, precision=None):
    return lax.dot_general(
        a, b, (((0,), (0,)), ((), ())), precision=precision, preferred_element_type=F32
    )


def halves(value):
    high = value.astype(BF16)
    return high, (value - high.astype(F32)).astype(BF16)


def dot3(a, b):
    ah, al = halves(a)
    bh, bl = halves(b)
    return dot(ah, bh) + (dot(ah, bl) + dot(al, bh))


def params(mib):
    return pltpu.CompilerParams(vmem_limit_bytes=mib * MIB)


def in_vmem(value):
    return pltpu.with_memory_space_constraint(value, pltpu.VMEM)


def in_hbm(value):
    return pltpu.with_memory_space_constraint(value, pltpu.HBM)


VMEM = pl.BlockSpec(memory_space=pltpu.VMEM)
ANY = pl.BlockSpec(memory_space=pl.ANY)
SMEM = pl.BlockSpec(memory_space=pltpu.SMEM)


SMALL = pl.CostEstimate(flops=1, bytes_accessed=1, transcendentals=0)


LONG = pl.CostEstimate(flops=10**10, bytes_accessed=4 * MIB, transcendentals=0)


def chunk_at(where, first, i):
    side = jnp.where(lax.rem(i, 2) == 0, where[0], 1 - where[0])
    return 2 * lax.rem(where[3] + first + i // 2, 4) + side


def whole(shape):
    return pl.BlockSpec(shape, lambda *_: (0,) * len(shape))


def power_kernel(where, momentum, gradient, right, after, *refs):
    power = refs[:4]
    m, g, q, sems, q_sem = refs[4:]
    copies = []
    for i in range(4):
        source = pl.ds(pl.multiple_of(where[i] * CHUNK, 16), CHUNK)
        for j, (array, slots) in enumerate(((momentum, m), (gradient, g))):
            copy = pltpu.make_async_copy(array.at[source], slots.at[i], sems.at[i, j])
            copy.start()
            copies.append(copy)
        if i == 0:
            q_copy = pltpu.make_async_copy(right, q, q_sem)
            q_copy.start()
    for i in range(4):
        copies[2 * i].wait()
        copies[2 * i + 1].wait()
        if i == 0:
            q_copy.wait()
        power[i][...] = dot((m[i] + g[i].astype(F32)).astype(BF16), q[...])


def power_chunks(where, momentum, gradient, right, after):
    return pl.pallas_call(
        power_kernel,
        in_specs=[SMEM] + [ANY] * 4,
        out_specs=[VMEM] * 4,
        out_shape=[jax.ShapeDtypeStruct((CHUNK, RANK), F32)] * 4,
        scratch_shapes=[
            pltpu.VMEM((4, CHUNK, COLS), F32),
            pltpu.VMEM((4, CHUNK, COLS), BF16),
            pltpu.VMEM((COLS, RANK), BF16),
            pltpu.SemaphoreType.DMA((4, 2)),
            pltpu.SemaphoreType.DMA,
        ],
        compiler_params=params(24),
        cost_estimate=SMALL,
        name="power_chunks",
    )(where, in_hbm(momentum), in_hbm(gradient), in_hbm(right), after)


def lower_kernel(momentum, gradient, after, lowered):
    lowered[...] = (momentum[...] + gradient[...].astype(F32)).astype(BF16)


def lower(momentum, gradient, after):
    tile = pl.BlockSpec((CHUNK, COLS), lambda i: (i, 0))
    return pl.pallas_call(
        lower_kernel,
        grid=(8,),
        in_specs=[tile, tile, ANY],
        out_specs=tile,
        out_shape=pltpu.HBM((ROWS, COLS), BF16),
        compiler_params=params(16),
        cost_estimate=SMALL,
        name="lower",
    )(in_hbm(momentum), in_hbm(gradient), after)


def gram_kernel(where, own, other, out):
    def strip(lo, hi, at):
        total = dot_t(own[:, lo:hi], own[:, at : at + BLOCK], HIGHEST)
        return total + dot_t(other[:, lo:hi], other[:, at : at + BLOCK], HIGHEST)

    @pl.when(where[0] == 0)
    def _():
        out[0:128] = strip(0, 128, 0)
        out[128:640] = strip(0, 512, 384)

    @pl.when(where[0] == 1)
    def _():
        out[0:256] = strip(0, 256, 128)
        out[256:640] = strip(0, 384, 256)


def gram_part(core, own, other):
    return pl.pallas_call(
        gram_kernel,
        grid_spec=pltpu.PrefetchScalarGridSpec(
            num_scalar_prefetch=1,
            grid=(1,),
            in_specs=[whole((CHUNK, RANK))] * 2,
            out_specs=whole((640, BLOCK)),
        ),
        out_shape=jax.ShapeDtypeStruct((640, BLOCK), F32),
        compiler_params=params(16),
        cost_estimate=SMALL,
        name="gram_part",
    )(core.reshape(1), own, other)


def block_inverse(matrix, eye):
    rows = lax.broadcasted_iota(jnp.int32, (8, BLOCK), 0)
    tile = (8, BLOCK)
    A = [matrix[8 * g : 8 * g + 8, :] for g in range(16)]
    E = [eye[8 * g : 8 * g + 8, :] for g in range(16)]
    out = []
    for p in range(16):
        col = {}
        for g in range(p, 16):
            for k in range(8):
                col[g, k] = jnp.broadcast_to(A[g][:, 8 * p + k : 8 * p + k + 1], tile)
        one = {}
        for k in range(8):
            for l in range(k, 8):
                one[k, l] = jnp.broadcast_to(col[p, k][l : l + 1, :], tile)
        row_a = [jnp.broadcast_to(A[p][k : k + 1, :], tile) for k in range(8)]
        row_e = [jnp.broadcast_to(E[p][k : k + 1, :], tile) for k in range(8)]
        done = []
        for k in range(8):
            inv = 1.0 / one[k, k]
            mult = {l: one[k, l] * inv for l in range(k + 1, 8)}
            for i in range(k + 1, 8):
                for l in range(i, 8):
                    one[i, l] = one[i, l] - one[k, i] * mult[l]
            scaled_a = row_a[k] * inv
            scaled_e = row_e[k] * inv
            for l in range(k + 1, 8):
                row_a[l] = row_a[l] - row_a[k] * mult[l]
                row_e[l] = row_e[l] - row_e[k] * mult[l]
            for g in range(p + 1, 16):
                for l in range(k + 1, 8):
                    col[g, l] = col[g, l] - col[g, k] * mult[l]
                A[g] = A[g] - col[g, k] * scaled_a
                E[g] = E[g] - col[g, k] * scaled_e
            done.append(row_e[k] * lax.rsqrt(one[k, k]))
        tile_out = done[0]
        for k in range(1, 8):
            tile_out = jnp.where(rows == k, done[k], tile_out)
        out.append(tile_out)
    return jnp.concatenate(out, axis=0)


def eliminate(x_ref, a, e, starts):
    eye = (
        lax.broadcasted_iota(jnp.int32, (BLOCK, BLOCK), 0)
        == lax.broadcasted_iota(jnp.int32, (BLOCK, BLOCK), 1)
    ).astype(F32)
    for lo in starts:
        hi = lo + BLOCK
        inverse = block_inverse(a[lo:hi, lo:hi], eye)
        x_ref[lo:hi, lo:hi] = inverse
        if lo > 0:
            x_ref[lo:hi, :lo] = dot(inverse, e[lo:hi, :lo], HIGHEST)
        if hi < RANK:
            upper = dot(inverse, a[lo:hi, hi:], HIGHEST)
            a[hi:, hi:] = a[hi:, hi:] - dot_t(upper, upper, HIGHEST)
            e[hi:, :hi] = e[hi:, :hi] - dot_t(upper, x_ref[lo:hi, :hi], HIGHEST)


def first_kernel(where, mine, theirs, x_ref, a, e, strips):
    strips[where[0]] = mine[...]
    strips[1 - where[0]] = theirs[...]
    a[0:128, 0:128] = strips[0, 0:128]
    a[0:512, 384:512] = strips[0, 128:640]
    a[0:256, 128:256] = strips[1, 0:256]
    a[0:384, 256:384] = strips[1, 256:640]
    x_ref[...] = jnp.zeros_like(x_ref)
    e[...] = jnp.zeros_like(e)
    eliminate(x_ref, a, e, (0, 128))


def second_kernel(x_in, a_in, e_in, after, x_ref, high, low, a, e):
    x_ref[...] = x_in[...]
    a[256:, 256:] = a_in[256:, 256:]
    e[256:, :] = e_in[256:, :]
    eliminate(x_ref, a, e, (256, 384))
    high[...], low[...] = halves(x_ref[...].T)


def inverse_first(where, mine, theirs):
    square = jax.ShapeDtypeStruct((RANK, RANK), F32)
    return pl.pallas_call(
        first_kernel,
        grid_spec=pltpu.PrefetchScalarGridSpec(
            num_scalar_prefetch=1,
            grid=(1,),
            in_specs=[whole((640, BLOCK))] * 2,
            out_specs=[whole((RANK, RANK))] * 3,
            scratch_shapes=[pltpu.VMEM((2, 640, BLOCK), F32)],
        ),
        out_shape=[square] * 3,
        compiler_params=params(24),
        cost_estimate=LONG,
        name="inverse_first",
    )(where, mine, theirs)


def inverse_second(state, after):
    square = jax.ShapeDtypeStruct((RANK, RANK), F32)
    return pl.pallas_call(
        second_kernel,
        grid=(1,),
        in_specs=[whole((RANK, RANK))] * 3 + [pl.BlockSpec(memory_space=pl.ANY)],
        out_specs=[whole((RANK, RANK))] * 3,
        out_shape=[square] + [jax.ShapeDtypeStruct((RANK, RANK), BF16)] * 2,
        scratch_shapes=[pltpu.VMEM((RANK, RANK), F32)] * 2,
        compiler_params=params(24),
        cost_estimate=LONG,
        name="inverse_second",
    )(*state, after)


def ordered(chunk, rows, core, own, other):
    for value, side in ((own, core), (other, 1 - core)):
        chunk[pl.ds(pl.multiple_of(rows + side * CHUNK, 16), CHUNK), :] = value


def product_kernel(where, *refs):
    power_in, lowered = refs[0:8], refs[8]
    out = refs[10:14]
    power, low, total, sems = refs[14:]
    copies = []
    for i in range(8):
        rows = pl.ds((i % 2) * CHUNK, CHUNK)
        at = pl.multiple_of(chunk_at(where, 0, 2 * ORDER[i // 2] + i % 2) * CHUNK, 16)
        source = lowered.at[pl.ds(at, CHUNK)]
        for j, (source, target) in enumerate(((power_in[i], power), (source, low))):
            copy = pltpu.make_async_copy(source, target.at[i // 2, rows], sems.at[i, j])
            copy.start()
            copies.append(copy)
    for i in range(4):
        for copy in copies[4 * i : 4 * i + 4]:
            copy.wait()
        first, second = halves(power[i])
        for at in range(0, COLS, 256):
            tall = low[i, :, at : at + 256]
            value = dot_t(second, tall) + dot_t(first, tall)
            if i > 0:
                value = value + total[:, at : at + 256]
            total[:, at : at + 256] = value
    for step in range(4):
        rows = pl.multiple_of(lax.rem(where[1] + step, 4) * BLOCK, BLOCK)
        out[step][...] = total[pl.ds(rows, BLOCK), :]


def product(where, power, lowered, after):
    return pl.pallas_call(
        product_kernel,
        in_specs=[SMEM] + [ANY] * 10,
        out_specs=[VMEM] * 4,
        out_shape=[jax.ShapeDtypeStruct((BLOCK, COLS), F32)] * 4,
        scratch_shapes=[
            pltpu.VMEM((4, PAIR, RANK), F32),
            pltpu.VMEM((4, PAIR, COLS), BF16),
            pltpu.VMEM((RANK, COLS), F32),
            pltpu.SemaphoreType.DMA((8, 2)),
        ],
        compiler_params=params(28),
        cost_estimate=SMALL,
        name="product",
    )(where, *[in_hbm(v) for v in power], in_hbm(lowered), after)


def cross_kernel(where, p0, p1, p2, p3, x_ref, cross_low, cross, colsq, total):
    first = where[1]
    for step, piece in enumerate((p0, p1, p2, p3)):
        at = pl.multiple_of(lax.rem(first + step, 4) * BLOCK, BLOCK)
        total[pl.ds(at, BLOCK), :] = piece[...]
    half = RANK // 2
    value = jnp.concatenate(
        [dot3(x_ref[:half, :half], total[:half, :]), dot3(x_ref[half:, :], total[...])], axis=0
    )
    cross_low[...] = value.astype(BF16)
    turned = value.T
    cross[...] = turned
    colsq[...] = jnp.sum(turned * turned, axis=0, keepdims=True)


def cross_of(where, pieces, x):
    return pl.pallas_call(
        cross_kernel,
        grid_spec=pltpu.PrefetchScalarGridSpec(
            num_scalar_prefetch=1,
            grid=(1,),
            in_specs=[whole((BLOCK, COLS))] * 4 + [whole((RANK, RANK))],
            out_specs=[whole((RANK, COLS)), whole((COLS, RANK)), whole((1, RANK))],
            scratch_shapes=[pltpu.VMEM((RANK, COLS), F32)],
        ),
        out_shape=[
            jax.ShapeDtypeStruct((RANK, COLS), BF16),
            jax.ShapeDtypeStruct((COLS, RANK), F32),
            jax.ShapeDtypeStruct((1, RANK), F32),
        ],
        compiler_params=params(40),
        cost_estimate=SMALL,
        name="cross_of",
    )(where, *pieces, x)


def update_kernel(n, first, where, momentum, gradient, xt_high, xt_low, cross_low, *refs):
    own, other = refs[:n], refs[n : 2 * n]
    left, momentum_next, chunk = refs[-3:]
    step = pl.program_id(0)
    for i in range(2 * n):

        @pl.when(step == i)
        def _():
            chunk[...] = (own, other)[i % 2][i // 2][...]

    high, low = halves(chunk[...])
    half = RANK // 2
    parts = []
    for rows, cols in ((half, slice(0, half)), (RANK, slice(half, RANK))):
        a, b = xt_high[:rows, cols], xt_low[:rows, cols]
        parts.append(dot(high[:, :rows], a) + (dot(high[:, :rows], b) + dot(low[:, :rows], a)))
    ortho = jnp.concatenate(parts, axis=1)
    left[...] = ortho * jnp.sqrt(F32(FF))
    feedback = dot(ortho.astype(BF16), cross_low[...])
    rows = pl.ds(pl.multiple_of(chunk_at(where, first, step) * CHUNK, 32), CHUNK)
    momentum_next[...] = (momentum[rows] + gradient[rows].astype(F32)) - 0.05 * feedback


def update(where, first, momentum, gradient, xt, cross_low, own, other, so_far=()):
    n = len(own)
    rows = lambda i, where: (chunk_at(where, first, i), 0)
    return pl.pallas_call(
        functools.partial(update_kernel, n, first),
        grid_spec=pltpu.PrefetchScalarGridSpec(
            num_scalar_prefetch=1,
            grid=(2 * n,),
            in_specs=[VMEM] * (5 + 2 * n) + [ANY] * len(so_far),
            out_specs=[pl.BlockSpec((CHUNK, RANK), rows), pl.BlockSpec((CHUNK, COLS), rows)],
            scratch_shapes=[pltpu.VMEM((CHUNK, RANK), F32)],
        ),
        out_shape=[
            jax.ShapeDtypeStruct((ROWS, RANK), F32),
            jax.ShapeDtypeStruct((ROWS, COLS), F32),
        ],
        input_output_aliases={6 + 2 * n + i: i for i in range(len(so_far))},
        compiler_params=params(20),
        cost_estimate=SMALL,
        name="update",
    )(
        where,
        in_vmem(momentum),
        in_vmem(gradient),
        *xt,
        cross_low,
        *[in_vmem(value) for value in (*own, *other)],
        *so_far,
    )


def on_device(momentum, gradient, right_factor):
    row = lax.axis_index("row")
    col = lax.axis_index("col")
    x, z, y, core = row // 4, row % 4, col // 2, col % 2
    first = jnp.where(core == 0, x, z)
    second = jnp.where(core == 0, z, x)
    where = jnp.stack([core, first, second, y]).astype(jnp.int32)

    def chunks(side):
        return jnp.stack([2 * ((y + step) % 4) + side for step in ORDER]).astype(jnp.int32)

    asked = power_chunks(chunks(1 - core), momentum, gradient, right_factor, right_factor)
    received = [to_partner(value) for value in asked]
    kept = power_chunks(chunks(core), momentum, gradient, right_factor, asked[0])
    terms = {step: kept[i] + received[i] for i, step in enumerate(ORDER)}
    got = [along_y(terms[step], step) for step in (2, 1, 3)]
    lowered = lower(momentum, gradient, terms[3])
    own = total_of(terms[0], got, lowered)
    other = to_partner(own)
    own_all = gathered(own, along_y)

    gram = gram_part(core, own, other)
    gram_1 = exchanged_sum(gram, along_first, (own_all[1], own_all[3]))

    got = [along_second(gram_1, step) for step in (2, 1, 3)]
    mine = [own] + [tied(own_all[i], got if i == 2 else gram_1) for i in (1, 2, 3)]
    theirs = [other] + [to_partner(piece) for piece in mine[1:]]
    power = [half[step] for step in ORDER for half in (mine, theirs)]
    turned = product(where, power, lowered, gram_1)

    gram_2 = total_of(gram_1, got, None)
    gram_3 = exchanged_sum(gram_2, along_y)
    turned = scattered_sum(turned, along_first, gram_3)
    state = inverse_first(where, tied(gram_3, turned), to_partner(gram_3))
    turned = exchanged_sum(turned, along_second, state[0])
    pieces = gathered(turned, along_first)

    inverse, *inverse_t = inverse_second(state, turned)
    pieces = [tied(piece, inverse) for piece in pieces]
    cross_low, cross, colsq = cross_of(where, pieces, inverse)

    def updated(steps, so_far=()):
        return update(
            where,
            steps[0],
            momentum,
            gradient,
            inverse_t,
            cross_low,
            [mine[step] for step in steps],
            [theirs[step] for step in steps],
            so_far,
        )

    results = updated((0, 1))
    colsq = exchanged_sum(colsq, along_y, results[0])
    colsq = colsq + to_partner(colsq)
    left_factor, momentum_next = updated((2, 3), results)
    colsq = tied(colsq, left_factor)
    right_next = (cross / jnp.sqrt(colsq / D + 1e-06)).astype(BF16)
    return (left_factor, momentum_next, right_next)


def solution(mesh):
    in_specs = (P("row", "col"), P("row", "col"), P("col", None))
    out_specs = (P("row", None), P("row", "col"), P("col", None))
    return jax.shard_map(
        on_device, mesh=mesh, in_specs=in_specs, out_specs=out_specs, check_vma=False
    )
```

```python
import functools

import jax
import jax.numpy as jnp
from jax import lax
from jax.experimental import pallas as pl
from jax.experimental.pallas import tpu as pltpu
from jax.sharding import PartitionSpec as P

FF = 28672
D = 8192
RANK = 512
ROWS = 1792
COLS = 1024
CHUNK = 224
PAIR = 448
ORDER = (2, 1, 3, 0)
BLOCK = 128
AXES = ("row", "col")
HIGHEST = lax.Precision.HIGHEST
MIB = 2**20
F32 = jnp.float32
BF16 = jnp.bfloat16


def place(x, z, y, core):
    return (x * 4 + z) * 8 + y * 2 + core


def pairs_of(move):
    out = []
    for x in range(4):
        for z in range(4):
            for y in range(4):
                for core in range(2):
                    out.append((place(x, z, y, core), place(*move(x, z, y, core))))
    return out


def to_partner(value):
    return lax.ppermute(value, AXES, pairs_of(lambda x, z, y, core: (x, z, y, 1 - core)))


def along_y(value, step):
    return lax.ppermute(value, AXES, pairs_of(lambda x, z, y, core: (x, z, (y + step) % 4, core)))


def along_first(value, step):
    def move(x, z, y, core):
        return ((x + step) % 4, z, y, core) if core == 0 else (x, (z + step) % 4, y, core)

    return lax.ppermute(value, AXES, pairs_of(move))


def along_second(value, step):
    def move(x, z, y, core):
        return (x, (z + step) % 4, y, core) if core == 0 else ((x + step) % 4, z, y, core)

    return lax.ppermute(value, AXES, pairs_of(move))


def tied(value, after):
    return value if after is None else lax.optimization_barrier((value, after))[0]


def total_of(own, got, after):
    got = [tied(part, after) for part in got]
    return (own + got[0]) + (got[1] + got[2])


def scattered_sum(blocks, along, after=None):
    return total_of(blocks[0], [along(blocks[step], step) for step in (2, 1, 3)], after)


def exchanged_sum(value, along, after=None):
    return total_of(value, [along(value, step) for step in (2, 1, 3)], after)


def gathered(value, along):
    got = {step: along(value, -step) for step in (2, 1, 3)}
    return [value, got[1], got[2], got[3]]


def dot(a, b, precision=None):
    return lax.dot_general(
        a, b, (((1,), (0,)), ((), ())), precision=precision, preferred_element_type=F32
    )


def dot_t(a, b, precision=None):
    return lax.dot_general(
        a, b, (((0,), (0,)), ((), ())), precision=precision, preferred_element_type=F32
    )


def halves(value):
    high = value.astype(BF16)
    return high, (value - high.astype(F32)).astype(BF16)


def dot3(a, b):
    ah, al = halves(a)
    bh, bl = halves(b)
    return dot(ah, bh) + (dot(ah, bl) + dot(al, bh))


def params(mib):
    return pltpu.CompilerParams(vmem_limit_bytes=mib * MIB)


def in_vmem(value):
    return pltpu.with_memory_space_constraint(value, pltpu.VMEM)


def in_hbm(value):
    return pltpu.with_memory_space_constraint(value, pltpu.HBM)


VMEM = pl.BlockSpec(memory_space=pltpu.VMEM)
ANY = pl.BlockSpec(memory_space=pl.ANY)
SMEM = pl.BlockSpec(memory_space=pltpu.SMEM)


SMALL = pl.CostEstimate(flops=1, bytes_accessed=1, transcendentals=0)


LONG = pl.CostEstimate(flops=10**10, bytes_accessed=4 * MIB, transcendentals=0)


def chunk_at(where, first, i):
    side = jnp.where(lax.rem(i, 2) == 0, where[0], 1 - where[0])
    return 2 * lax.rem(where[3] + first + i // 2, 4) + side


def whole(shape):
    return pl.BlockSpec(shape, lambda *_: (0,) * len(shape))


def power_kernel(where, momentum, gradient, right, after, *refs):
    power = refs[:4]
    m, g, q, sems, q_sem = refs[4:]
    copies = []
    for i in range(4):
        source = pl.ds(pl.multiple_of(where[i] * CHUNK, 16), CHUNK)
        for j, (array, slots) in enumerate(((momentum, m), (gradient, g))):
            copy = pltpu.make_async_copy(array.at[source], slots.at[i], sems.at[i, j])
            copy.start()
            copies.append(copy)
        if i == 0:
            q_copy = pltpu.make_async_copy(right, q, q_sem)
            q_copy.start()
    for i in range(4):
        copies[2 * i].wait()
        copies[2 * i + 1].wait()
        if i == 0:
            q_copy.wait()
        power[i][...] = dot((m[i] + g[i].astype(F32)).astype(BF16), q[...])


def power_chunks(where, momentum, gradient, right, after):
    return pl.pallas_call(
        power_kernel,
        in_specs=[SMEM] + [ANY] * 4,
        out_specs=[VMEM] * 4,
        out_shape=[jax.ShapeDtypeStruct((CHUNK, RANK), F32)] * 4,
        scratch_shapes=[
            pltpu.VMEM((4, CHUNK, COLS), F32),
            pltpu.VMEM((4, CHUNK, COLS), BF16),
            pltpu.VMEM((COLS, RANK), BF16),
            pltpu.SemaphoreType.DMA((4, 2)),
            pltpu.SemaphoreType.DMA,
        ],
        compiler_params=params(24),
        cost_estimate=SMALL,
        name="power_chunks",
    )(where, in_hbm(momentum), in_hbm(gradient), in_hbm(right), after)


def lower_kernel(momentum, gradient, after, lowered):
    lowered[...] = (momentum[...] + gradient[...].astype(F32)).astype(BF16)


def lower(momentum, gradient, after):
    tile = pl.BlockSpec((CHUNK, COLS), lambda i: (i, 0))
    return pl.pallas_call(
        lower_kernel,
        grid=(8,),
        in_specs=[tile, tile, ANY],
        out_specs=tile,
        out_shape=pltpu.HBM((ROWS, COLS), BF16),
        compiler_params=params(16),
        cost_estimate=SMALL,
        name="lower",
    )(in_hbm(momentum), in_hbm(gradient), after)


def gram_kernel(where, own, other, out):
    def strip(lo, hi, at):
        total = dot_t(own[:, lo:hi], own[:, at : at + BLOCK], HIGHEST)
        return total + dot_t(other[:, lo:hi], other[:, at : at + BLOCK], HIGHEST)

    @pl.when(where[0] == 0)
    def _():
        out[0:128] = strip(0, 128, 0)
        out[128:640] = strip(0, 512, 384)

    @pl.when(where[0] == 1)
    def _():
        out[0:256] = strip(0, 256, 128)
        out[256:640] = strip(0, 384, 256)


def gram_part(core, own, other):
    return pl.pallas_call(
        gram_kernel,
        grid_spec=pltpu.PrefetchScalarGridSpec(
            num_scalar_prefetch=1,
            grid=(1,),
            in_specs=[whole((CHUNK, RANK))] * 2,
            out_specs=whole((640, BLOCK)),
        ),
        out_shape=jax.ShapeDtypeStruct((640, BLOCK), F32),
        compiler_params=params(16),
        cost_estimate=SMALL,
        name="gram_part",
    )(core.reshape(1), own, other)


def block_inverse(matrix, beside=()):
    beside = list(beside)
    tile = (8, BLOCK)
    rows = lax.broadcasted_iota(jnp.int32, tile, 0)
    lanes = lax.broadcasted_iota(jnp.int32, tile, 1)
    W = [matrix[8 * g : 8 * g + 8, :] for g in range(16)]
    out = []

    def columns(value, at):
        return [jnp.broadcast_to(value[:, at + k : at + k + 1], tile) for k in range(8)]

    for p in range(16):
        at = 8 * p
        col = columns(W[p], at)
        one = {(k, l): jnp.broadcast_to(col[k][l : l + 1, :], tile) for k in range(8) for l in range(k, 8)}
        panel = (lanes >= at) & (lanes < at + 8)
        own = jnp.where(panel, (lanes - at == rows).astype(F32), W[p])
        row = [jnp.broadcast_to(own[k : k + 1, :], tile) for k in range(8)]
        done, steps = [], []
        for k in range(0, 8, 2):
            a, b, d = one[k, k], one[k, k + 1], one[k + 1, k + 1]
            det = a * d - b * b
            inv = 1.0 / det
            u, v = {}, {}
            for l in range(k + 2, 8):
                u[l] = (d * one[k, l] - b * one[k + 1, l]) * inv
                v[l] = (a * one[k + 1, l] - b * one[k, l]) * inv
            for i in range(k + 2, 8):
                for l in range(i, 8):
                    one[i, l] = one[i, l] - (one[k, i] * u[l] + one[k + 1, i] * v[l])
            r, s = row[k], row[k + 1]
            for l in range(k + 2, 8):
                row[l] = row[l] - (r * u[l] + s * v[l])
            steps.append((k, u, v, (d * r - b * s) * inv, (a * s - b * r) * inv))
            inv_a = 1.0 / a
            done.append(r * lax.rsqrt(a))
            done.append((s - r * (b * inv_a)) * lax.rsqrt(det * inv_a))
        result = done[0]
        for k in range(1, 8):
            result = jnp.where(rows == k, done[k], result)
        out.append(jnp.where(lanes < at + 8, result, 0.0))
        for g in range(p + 1, 16):
            col = columns(W[g], at)
            total = None
            for k, u, v, first, second in steps:
                term = col[k] * first + col[k + 1] * second
                total = term if total is None else total + term
                for l in range(k + 2, 8):
                    col[l] = col[l] - (col[k] * u[l] + col[k + 1] * v[l])
            W[g] = jnp.where(panel, 0.0, W[g]) - total
        if beside and p % 2 == 1:
            beside.pop(0)()
    for step in beside:
        step()
    return jnp.concatenate(out, axis=0)


def eliminate(x_ref, a, e, starts):
    for lo in starts:
        hi, before = lo + BLOCK, lo - BLOCK
        diagonal = a[lo:hi, lo:hi]
        beside = []
        if lo > 0:
            last = x_ref[before:lo, before:lo]
            upper = {lo: dot(last, a[before:lo, lo:hi], HIGHEST)}
            diagonal = diagonal - dot_t(upper[lo], upper[lo], HIGHEST)

            def strip(at):
                def step():
                    upper[at] = dot(last, a[before:lo, at : at + BLOCK], HIGHEST)
                    for row in range(lo, at + BLOCK, BLOCK):
                        block = (slice(row, row + BLOCK), slice(at, at + BLOCK))
                        a[block] = a[block] - dot_t(upper[row], upper[at], HIGHEST)

                return step

            def rows_of_e(at):
                def step():
                    block = (slice(at, at + BLOCK), slice(0, lo))
                    e[block] = e[block] - dot_t(upper[at], x_ref[before:lo, :lo], HIGHEST)

                return step

            beside = [rows_of_e(lo)]
            for at in range(hi, RANK, BLOCK):
                beside += [strip(at), rows_of_e(at)]
        inverse = block_inverse(diagonal, beside)
        x_ref[lo:hi, lo:hi] = inverse
        if lo > 0:
            x_ref[lo:hi, :lo] = dot(inverse, e[lo:hi, :lo], HIGHEST)


def first_kernel(where, mine, theirs, x_ref, a, e, strips):
    strips[where[0]] = mine[...]
    strips[1 - where[0]] = theirs[...]
    a[0:128, 0:128] = strips[0, 0:128]
    a[0:512, 384:512] = strips[0, 128:640]
    a[0:256, 128:256] = strips[1, 0:256]
    a[0:384, 256:384] = strips[1, 256:640]
    x_ref[...] = jnp.zeros_like(x_ref)
    e[...] = jnp.zeros_like(e)
    eliminate(x_ref, a, e, (0, 128, 256))


def second_kernel(x_in, a_in, e_in, after, x_ref, high, low, a, e):
    x_ref[...] = x_in[...]
    a[256:, 384:] = a_in[256:, 384:]
    e[384:, :] = e_in[384:, :]
    eliminate(x_ref, a, e, (384,))
    high[...], low[...] = halves(x_ref[...].T)


def inverse_first(where, mine, theirs):
    square = jax.ShapeDtypeStruct((RANK, RANK), F32)
    return pl.pallas_call(
        first_kernel,
        grid_spec=pltpu.PrefetchScalarGridSpec(
            num_scalar_prefetch=1,
            grid=(1,),
            in_specs=[whole((640, BLOCK))] * 2,
            out_specs=[whole((RANK, RANK))] * 3,
            scratch_shapes=[pltpu.VMEM((2, 640, BLOCK), F32)],
        ),
        out_shape=[square] * 3,
        compiler_params=params(24),
        cost_estimate=LONG,
        name="inverse_first",
    )(where, mine, theirs)


def inverse_second(state, after):
    square = jax.ShapeDtypeStruct((RANK, RANK), F32)
    return pl.pallas_call(
        second_kernel,
        grid=(1,),
        in_specs=[whole((RANK, RANK))] * 3 + [pl.BlockSpec(memory_space=pl.ANY)],
        out_specs=[whole((RANK, RANK))] * 3,
        out_shape=[square] + [jax.ShapeDtypeStruct((RANK, RANK), BF16)] * 2,
        scratch_shapes=[pltpu.VMEM((RANK, RANK), F32)] * 2,
        compiler_params=params(24),
        cost_estimate=LONG,
        name="inverse_second",
    )(*state, after)


def ordered(chunk, rows, core, own, other):
    for value, side in ((own, core), (other, 1 - core)):
        chunk[pl.ds(pl.multiple_of(rows + side * CHUNK, 16), CHUNK), :] = value


def product_kernel(where, *refs):
    power_in, lowered = refs[0:8], refs[8]
    out = refs[-8:-4]
    power, low, total, sems = refs[-4:]
    copies = []
    for i in range(8):
        rows = pl.ds((i % 2) * CHUNK, CHUNK)
        at = pl.multiple_of(chunk_at(where, 0, 2 * ORDER[i // 2] + i % 2) * CHUNK, 16)
        source = lowered.at[pl.ds(at, CHUNK)]
        for j, (source, target) in enumerate(((power_in[i], power), (source, low))):
            copy = pltpu.make_async_copy(source, target.at[i // 2, rows], sems.at[i, j])
            copy.start()
            copies.append(copy)
    for i in range(4):
        for copy in copies[4 * i : 4 * i + 4]:
            copy.wait()
        first, second = halves(power[i])
        for at in range(0, COLS, 256):
            tall = low[i, :, at : at + 256]
            value = dot_t(second, tall) + dot_t(first, tall)
            if i > 0:
                value = value + total[:, at : at + 256]
            total[:, at : at + 256] = value
    for step in range(4):
        rows = pl.multiple_of(lax.rem(where[1] + step, 4) * BLOCK, BLOCK)
        out[step][...] = total[pl.ds(rows, BLOCK), :]


def product(where, power, lowered, after):
    return pl.pallas_call(
        product_kernel,
        in_specs=[SMEM] + [ANY] * (9 + len(after)),
        out_specs=[VMEM] * 4,
        out_shape=[jax.ShapeDtypeStruct((BLOCK, COLS), F32)] * 4,
        scratch_shapes=[
            pltpu.VMEM((4, PAIR, RANK), F32),
            pltpu.VMEM((4, PAIR, COLS), BF16),
            pltpu.VMEM((RANK, COLS), F32),
            pltpu.SemaphoreType.DMA((8, 2)),
        ],
        compiler_params=params(28),
        cost_estimate=SMALL,
        name="product",
    )(where, *[in_hbm(v) for v in power], in_hbm(lowered), *after)


def cross_kernel(where, p0, p1, p2, p3, x_ref, cross_low, cross, colsq, total):
    first = where[1]
    for step, piece in enumerate((p0, p1, p2, p3)):
        at = pl.multiple_of(lax.rem(first + step, 4) * BLOCK, BLOCK)
        total[pl.ds(at, BLOCK), :] = piece[...]
    half = RANK // 2
    value = jnp.concatenate(
        [dot3(x_ref[:half, :half], total[:half, :]), dot3(x_ref[half:, :], total[...])], axis=0
    )
    cross_low[...] = value.astype(BF16)
    turned = value.T
    cross[...] = turned
    colsq[...] = jnp.sum(turned * turned, axis=0, keepdims=True)


def cross_of(where, pieces, x):
    return pl.pallas_call(
        cross_kernel,
        grid_spec=pltpu.PrefetchScalarGridSpec(
            num_scalar_prefetch=1,
            grid=(1,),
            in_specs=[whole((BLOCK, COLS))] * 4 + [whole((RANK, RANK))],
            out_specs=[whole((RANK, COLS)), whole((COLS, RANK)), whole((1, RANK))],
            scratch_shapes=[pltpu.VMEM((RANK, COLS), F32)],
        ),
        out_shape=[
            jax.ShapeDtypeStruct((RANK, COLS), BF16),
            jax.ShapeDtypeStruct((COLS, RANK), F32),
            jax.ShapeDtypeStruct((1, RANK), F32),
        ],
        compiler_params=params(40),
        cost_estimate=SMALL,
        name="cross_of",
    )(where, *pieces, x)


def left_kernel(where, xt_high, xt_low, *refs):
    left, left_low, chunk = refs[-3:]
    for i in range(4):

        @pl.when(pl.program_id(0) == i)
        def _():
            for value, side in ((refs[2 * i], where[0]), (refs[2 * i + 1], 1 - where[0])):
                chunk[pl.ds(pl.multiple_of(side * CHUNK, 16), CHUNK), :] = value[...]

    high, low = halves(chunk[...])
    half = RANK // 2
    for rows, cols in ((half, slice(0, half)), (RANK, slice(half, RANK))):
        a, b = xt_high[:rows, cols], xt_low[:rows, cols]
        ortho = dot(high[:, :rows], a) + (dot(high[:, :rows], b) + dot(low[:, :rows], a))
        left[:, cols] = ortho * jnp.sqrt(F32(FF))
        left_low[:, cols] = ortho.astype(BF16)


def left_of(where, power, xt):
    tile = pl.BlockSpec((PAIR, RANK), lambda i, where: (lax.rem(where[3] + i, 4), 0))
    return pl.pallas_call(
        left_kernel,
        grid_spec=pltpu.PrefetchScalarGridSpec(
            num_scalar_prefetch=1,
            grid=(4,),
            in_specs=[VMEM] * 10,
            out_specs=[tile, tile],
            scratch_shapes=[pltpu.VMEM((PAIR, RANK), F32)],
        ),
        out_shape=[
            jax.ShapeDtypeStruct((ROWS, RANK), F32),
            jax.ShapeDtypeStruct((ROWS, RANK), BF16),
        ],
        compiler_params=params(16),
        cost_estimate=SMALL,
        name="left_of",
    )(where, *xt, *[in_vmem(value) for value in power])


def update_kernel(first, momentum, gradient, left_low, cross_low, *refs):
    feedback = dot(left_low[...], cross_low[...])
    at = (pl.program_id(0) + first) * CHUNK
    rows = pl.ds(pl.multiple_of(at, 32), CHUNK)
    refs[-1][...] = (momentum[rows] + gradient[rows].astype(F32)) - 0.05 * feedback


def update(first, momentum, gradient, left_low, cross_low, so_far=()):
    rows = lambda i: (i + first, 0)
    return pl.pallas_call(
        functools.partial(update_kernel, first),
        grid=(4,),
        in_specs=[VMEM, VMEM, pl.BlockSpec((CHUNK, RANK), rows), VMEM] + [ANY] * len(so_far),
        out_specs=pl.BlockSpec((CHUNK, COLS), rows),
        out_shape=jax.ShapeDtypeStruct((ROWS, COLS), F32),
        input_output_aliases={4: 0} if so_far else {},
        compiler_params=params(16),
        cost_estimate=SMALL,
        name="update",
    )(in_vmem(momentum), in_vmem(gradient), left_low, cross_low, *so_far)


def on_device(momentum, gradient, right_factor):
    row = lax.axis_index("row")
    col = lax.axis_index("col")
    x, z, y, core = row // 4, row % 4, col // 2, col % 2
    first = jnp.where(core == 0, x, z)
    second = jnp.where(core == 0, z, x)
    where = jnp.stack([core, first, second, y]).astype(jnp.int32)

    def chunks(side):
        return jnp.stack([2 * ((y + step) % 4) + side for step in ORDER]).astype(jnp.int32)

    asked = power_chunks(chunks(1 - core), momentum, gradient, right_factor, right_factor)
    received = [to_partner(value) for value in asked]
    kept = power_chunks(chunks(core), momentum, gradient, right_factor, asked[0])
    terms = {step: kept[i] + received[i] for i, step in enumerate(ORDER)}
    got = [along_y(terms[step], step) for step in (2, 1, 3)]
    lowered = lower(momentum, gradient, terms[3])
    own = total_of(terms[0], got, lowered)
    other = to_partner(own)
    own_all = gathered(own, along_y)

    gram = gram_part(core, own, other)
    gram_1 = exchanged_sum(gram, along_first, (own_all[1], own_all[3]))

    got = [along_second(gram_1, step) for step in (2, 1, 3)]
    mine = [own] + [tied(own_all[i], got if i == 2 else gram_1) for i in (1, 2, 3)]
    theirs = [other] + [to_partner(piece) for piece in mine[1:]]
    power = [half[step] for step in ORDER for half in (mine, theirs)]
    turned = product(where, power, lowered, [gram_1])

    gram_2 = total_of(gram_1, got, None)
    gram_3 = exchanged_sum(gram_2, along_y)
    turned = scattered_sum(turned, along_first, gram_3)
    state = inverse_first(where, tied(gram_3, turned), to_partner(gram_3))
    turned = exchanged_sum(turned, along_second, state[0])
    pieces = gathered(turned, along_first)

    inverse, *inverse_t = inverse_second(state, turned)
    power = [half[step] for step in range(4) for half in (mine, theirs)]
    left_factor, left_low = left_of(where, power, inverse_t)
    pieces = [tied(piece, left_low) for piece in pieces]
    cross_low, cross, colsq = cross_of(where, pieces, inverse)

    momentum_next = update(0, momentum, gradient, left_low, cross_low)
    colsq = exchanged_sum(colsq, along_y, momentum_next)
    colsq = colsq + to_partner(colsq)
    momentum_next = update(4, momentum, gradient, left_low, cross_low, (momentum_next,))
    colsq = tied(colsq, momentum_next)
    right_next = (cross / jnp.sqrt(colsq / D + 1e-06)).astype(BF16)
    return (left_factor, momentum_next, right_next)


def solution(mesh):
    in_specs = (P("row", "col"), P("row", "col"), P("col", None))
    out_specs = (P("row", None), P("row", "col"), P("col", None))
    return jax.shard_map(
        on_device, mesh=mesh, in_specs=in_specs, out_specs=out_specs, check_vma=False
    )
```

```python
import functools

import jax
import jax.numpy as jnp
from jax import lax
from jax.experimental import pallas as pl
from jax.experimental.pallas import tpu as pltpu
from jax.sharding import PartitionSpec as P

FF = 28672
D = 8192
RANK = 512
ROWS = 1792
COLS = 1024
CHUNK = 224
PAIR = 448
ORDER = (2, 1, 3, 0)
BLOCK = 128
AXES = ("row", "col")
HIGHEST = lax.Precision.HIGHEST
MIB = 2**20
F32 = jnp.float32
BF16 = jnp.bfloat16


def place(x, z, y, core):
    return (x * 4 + z) * 8 + y * 2 + core


def pairs_of(move):
    out = []
    for x in range(4):
        for z in range(4):
            for y in range(4):
                for core in range(2):
                    out.append((place(x, z, y, core), place(*move(x, z, y, core))))
    return out


def to_partner(value):
    return lax.ppermute(value, AXES, pairs_of(lambda x, z, y, core: (x, z, y, 1 - core)))


def along_y(value, step):
    return lax.ppermute(value, AXES, pairs_of(lambda x, z, y, core: (x, z, (y + step) % 4, core)))


def along_first(value, step):
    def move(x, z, y, core):
        return ((x + step) % 4, z, y, core) if core == 0 else (x, (z + step) % 4, y, core)

    return lax.ppermute(value, AXES, pairs_of(move))


def along_second(value, step):
    def move(x, z, y, core):
        return (x, (z + step) % 4, y, core) if core == 0 else ((x + step) % 4, z, y, core)

    return lax.ppermute(value, AXES, pairs_of(move))


def tied(value, after):
    return value if after is None else lax.optimization_barrier((value, after))[0]


def total_of(own, got, after):
    got = [tied(part, after) for part in got]
    return (own + got[0]) + (got[1] + got[2])


def scattered_sum(blocks, along, after=None):
    return total_of(blocks[0], [along(blocks[step], step) for step in (2, 1, 3)], after)


def exchanged_sum(value, along, after=None):
    return total_of(value, [along(value, step) for step in (2, 1, 3)], after)


def gathered(value, along):
    got = {step: along(value, -step) for step in (2, 1, 3)}
    return [value, got[1], got[2], got[3]]


def dot(a, b, precision=None):
    return lax.dot_general(
        a, b, (((1,), (0,)), ((), ())), precision=precision, preferred_element_type=F32
    )


def dot_t(a, b, precision=None):
    return lax.dot_general(
        a, b, (((0,), (0,)), ((), ())), precision=precision, preferred_element_type=F32
    )


def halves(value):
    high = value.astype(BF16)
    return high, (value - high.astype(F32)).astype(BF16)


def dot3(a, b):
    ah, al = halves(a)
    bh, bl = halves(b)
    return dot(ah, bh) + (dot(ah, bl) + dot(al, bh))


def params(mib):
    return pltpu.CompilerParams(vmem_limit_bytes=mib * MIB)


def in_vmem(value):
    return pltpu.with_memory_space_constraint(value, pltpu.VMEM)


def in_hbm(value):
    return pltpu.with_memory_space_constraint(value, pltpu.HBM)


VMEM = pl.BlockSpec(memory_space=pltpu.VMEM)
ANY = pl.BlockSpec(memory_space=pl.ANY)
SMEM = pl.BlockSpec(memory_space=pltpu.SMEM)


SMALL = pl.CostEstimate(flops=1, bytes_accessed=1, transcendentals=0)


LONG = pl.CostEstimate(flops=10**10, bytes_accessed=4 * MIB, transcendentals=0)


def chunk_at(where, first, i):
    side = jnp.where(lax.rem(i, 2) == 0, where[0], 1 - where[0])
    return 2 * lax.rem(where[3] + first + i // 2, 4) + side


def whole(shape):
    return pl.BlockSpec(shape, lambda *_: (0,) * len(shape))


def power_kernel(where, momentum, gradient, right, after, *refs):
    power = refs[:4]
    m, g, q, sems, q_sem = refs[4:]
    copies = []
    for i in range(4):
        source = pl.ds(pl.multiple_of(where[i] * CHUNK, 16), CHUNK)
        for j, (array, slots) in enumerate(((momentum, m), (gradient, g))):
            copy = pltpu.make_async_copy(array.at[source], slots.at[i], sems.at[i, j])
            copy.start()
            copies.append(copy)
        if i == 0:
            q_copy = pltpu.make_async_copy(right, q, q_sem)
            q_copy.start()
    for i in range(4):
        copies[2 * i].wait()
        copies[2 * i + 1].wait()
        if i == 0:
            q_copy.wait()
        power[i][...] = dot((m[i] + g[i].astype(F32)).astype(BF16), q[...])


def power_chunks(where, momentum, gradient, right, after):
    return pl.pallas_call(
        power_kernel,
        in_specs=[SMEM] + [ANY] * 4,
        out_specs=[VMEM] * 4,
        out_shape=[jax.ShapeDtypeStruct((CHUNK, RANK), F32)] * 4,
        scratch_shapes=[
            pltpu.VMEM((4, CHUNK, COLS), F32),
            pltpu.VMEM((4, CHUNK, COLS), BF16),
            pltpu.VMEM((COLS, RANK), BF16),
            pltpu.SemaphoreType.DMA((4, 2)),
            pltpu.SemaphoreType.DMA,
        ],
        compiler_params=params(24),
        cost_estimate=SMALL,
        name="power_chunks",
    )(where, in_hbm(momentum), in_hbm(gradient), in_hbm(right), after)


def lower_kernel(momentum, gradient, after, lowered):
    lowered[...] = (momentum[...] + gradient[...].astype(F32)).astype(BF16)


def lower(momentum, gradient, after):
    tile = pl.BlockSpec((CHUNK, COLS), lambda i: (i, 0))
    return pl.pallas_call(
        lower_kernel,
        grid=(8,),
        in_specs=[tile, tile, ANY],
        out_specs=tile,
        out_shape=pltpu.HBM((ROWS, COLS), BF16),
        compiler_params=params(16),
        cost_estimate=SMALL,
        name="lower",
    )(in_hbm(momentum), in_hbm(gradient), after)


def gram_kernel(where, own, other, out):
    def strip(lo, hi, at):
        total = dot_t(own[:, lo:hi], own[:, at : at + BLOCK], HIGHEST)
        return total + dot_t(other[:, lo:hi], other[:, at : at + BLOCK], HIGHEST)

    @pl.when(where[0] == 0)
    def _():
        out[0:128] = strip(0, 128, 0)
        out[128:640] = strip(0, 512, 384)

    @pl.when(where[0] == 1)
    def _():
        out[0:256] = strip(0, 256, 128)
        out[256:640] = strip(0, 384, 256)


def gram_part(core, own, other):
    return pl.pallas_call(
        gram_kernel,
        grid_spec=pltpu.PrefetchScalarGridSpec(
            num_scalar_prefetch=1,
            grid=(1,),
            in_specs=[whole((CHUNK, RANK))] * 2,
            out_specs=whole((640, BLOCK)),
        ),
        out_shape=jax.ShapeDtypeStruct((640, BLOCK), F32),
        compiler_params=params(16),
        cost_estimate=SMALL,
        name="gram_part",
    )(core.reshape(1), own, other)


def block_inverse(matrix, beside=()):
    beside = list(beside)
    tile = (8, BLOCK)
    rows = lax.broadcasted_iota(jnp.int32, tile, 0)
    lanes = lax.broadcasted_iota(jnp.int32, tile, 1)
    W = [matrix[8 * g : 8 * g + 8, :] for g in range(16)]
    out = []

    def columns(value, at):
        return [jnp.broadcast_to(value[:, at + k : at + k + 1], tile) for k in range(8)]

    for p in range(16):
        at = 8 * p
        col = columns(W[p], at)
        one = {(k, l): jnp.broadcast_to(col[k][l : l + 1, :], tile) for k in range(8) for l in range(k, 8)}
        panel = (lanes >= at) & (lanes < at + 8)
        own = jnp.where(panel, (lanes - at == rows).astype(F32), W[p])
        row = [jnp.broadcast_to(own[k : k + 1, :], tile) for k in range(8)]
        done, steps = [], []
        for k in range(0, 8, 2):
            a, b, d = one[k, k], one[k, k + 1], one[k + 1, k + 1]
            det = a * d - b * b
            inv = 1.0 / det
            u, v = {}, {}
            for l in range(k + 2, 8):
                u[l] = (d * one[k, l] - b * one[k + 1, l]) * inv
                v[l] = (a * one[k + 1, l] - b * one[k, l]) * inv
            for i in range(k + 2, 8):
                for l in range(i, 8):
                    one[i, l] = one[i, l] - (one[k, i] * u[l] + one[k + 1, i] * v[l])
            r, s = row[k], row[k + 1]
            for l in range(k + 2, 8):
                row[l] = row[l] - (r * u[l] + s * v[l])
            steps.append((k, u, v, (d * r - b * s) * inv, (a * s - b * r) * inv))
            inv_a = 1.0 / a
            done.append(r * lax.rsqrt(a))
            done.append((s - r * (b * inv_a)) * lax.rsqrt(det * inv_a))
        result = done[0]
        for k in range(1, 8):
            result = jnp.where(rows == k, done[k], result)
        out.append(jnp.where(lanes < at + 8, result, 0.0))
        for g in range(p + 1, 16):
            col = columns(W[g], at)
            total = None
            for k, u, v, first, second in steps:
                term = col[k] * first + col[k + 1] * second
                total = term if total is None else total + term
                for l in range(k + 2, 8):
                    col[l] = col[l] - (col[k] * u[l] + col[k + 1] * v[l])
            W[g] = jnp.where(panel, 0.0, W[g]) - total
        if beside and p % 2 == 1:
            beside.pop(0)()
    for step in beside:
        step()
    return jnp.concatenate(out, axis=0)


def eliminate(x_ref, a, e, starts):
    for lo in starts:
        hi, before = lo + BLOCK, lo - BLOCK
        diagonal = a[lo:hi, lo:hi]
        beside = []
        if lo > 0:
            last = x_ref[before:lo, before:lo]
            upper = {lo: dot(last, a[before:lo, lo:hi], HIGHEST)}
            diagonal = diagonal - dot_t(upper[lo], upper[lo], HIGHEST)

            def strip(at):
                def step():
                    upper[at] = dot(last, a[before:lo, at : at + BLOCK], HIGHEST)
                    for row in range(lo, at + BLOCK, BLOCK):
                        block = (slice(row, row + BLOCK), slice(at, at + BLOCK))
                        a[block] = a[block] - dot_t(upper[row], upper[at], HIGHEST)

                return step

            def rows_of_e(at):
                def step():
                    block = (slice(at, at + BLOCK), slice(0, lo))
                    e[block] = e[block] - dot_t(upper[at], x_ref[before:lo, :lo], HIGHEST)

                return step

            beside = [rows_of_e(lo)]
            for at in range(hi, RANK, BLOCK):
                beside += [strip(at), rows_of_e(at)]
        inverse = block_inverse(diagonal, beside)
        x_ref[lo:hi, lo:hi] = inverse
        if lo > 0:
            x_ref[lo:hi, :lo] = dot(inverse, e[lo:hi, :lo], HIGHEST)


def first_kernel(where, mine, theirs, x_ref, a, e, strips):
    strips[where[0]] = mine[...]
    strips[1 - where[0]] = theirs[...]
    a[0:128, 0:128] = strips[0, 0:128]
    a[0:512, 384:512] = strips[0, 128:640]
    a[0:256, 128:256] = strips[1, 0:256]
    a[0:384, 256:384] = strips[1, 256:640]
    x_ref[...] = jnp.zeros_like(x_ref)
    e[...] = jnp.zeros_like(e)
    eliminate(x_ref, a, e, (0, 128, 256))


def second_kernel(x_in, a_in, e_in, after, x_ref, high, low, a, e):
    x_ref[...] = x_in[...]
    a[256:, 384:] = a_in[256:, 384:]
    e[384:, :] = e_in[384:, :]
    eliminate(x_ref, a, e, (384,))
    high[...], low[...] = halves(x_ref[...].T)


def inverse_first(where, mine, theirs):
    square = jax.ShapeDtypeStruct((RANK, RANK), F32)
    return pl.pallas_call(
        first_kernel,
        grid_spec=pltpu.PrefetchScalarGridSpec(
            num_scalar_prefetch=1,
            grid=(1,),
            in_specs=[whole((640, BLOCK))] * 2,
            out_specs=[whole((RANK, RANK))] * 3,
            scratch_shapes=[pltpu.VMEM((2, 640, BLOCK), F32)],
        ),
        out_shape=[square] * 3,
        compiler_params=params(24),
        cost_estimate=LONG,
        name="inverse_first",
    )(where, mine, theirs)


def inverse_second(state, after):
    square = jax.ShapeDtypeStruct((RANK, RANK), F32)
    return pl.pallas_call(
        second_kernel,
        grid=(1,),
        in_specs=[whole((RANK, RANK))] * 3 + [pl.BlockSpec(memory_space=pl.ANY)],
        out_specs=[whole((RANK, RANK))] * 3,
        out_shape=[square] + [jax.ShapeDtypeStruct((RANK, RANK), BF16)] * 2,
        scratch_shapes=[pltpu.VMEM((RANK, RANK), F32)] * 2,
        compiler_params=params(24),
        cost_estimate=LONG,
        name="inverse_second",
    )(*state, after)


def ordered(chunk, rows, core, own, other):
    for value, side in ((own, core), (other, 1 - core)):
        chunk[pl.ds(pl.multiple_of(rows + side * CHUNK, 16), CHUNK), :] = value


def product_kernel(where, *refs):
    power_in, lowered = refs[0:8], refs[8]
    out = refs[-8:-4]
    power, low, total, sems = refs[-4:]
    copies = []
    for i in range(8):
        rows = pl.ds((i % 2) * CHUNK, CHUNK)
        at = pl.multiple_of(chunk_at(where, 0, 2 * ORDER[i // 2] + i % 2) * CHUNK, 16)
        source = lowered.at[pl.ds(at, CHUNK)]
        for j, (source, target) in enumerate(((power_in[i], power), (source, low))):
            copy = pltpu.make_async_copy(source, target.at[i // 2, rows], sems.at[i, j])
            copy.start()
            copies.append(copy)
    for i in range(4):
        for copy in copies[4 * i : 4 * i + 4]:
            copy.wait()
        first, second = halves(power[i])
        for at in range(0, COLS, 256):
            tall = low[i, :, at : at + 256]
            value = dot_t(second, tall) + dot_t(first, tall)
            if i > 0:
                value = value + total[:, at : at + 256]
            total[:, at : at + 256] = value
    for step in range(4):
        rows = pl.multiple_of(lax.rem(where[1] + step, 4) * BLOCK, BLOCK)
        out[step][...] = total[pl.ds(rows, BLOCK), :]


def product(where, power, lowered, after):
    return pl.pallas_call(
        product_kernel,
        in_specs=[SMEM] + [ANY] * (9 + len(after)),
        out_specs=[VMEM] * 4,
        out_shape=[jax.ShapeDtypeStruct((BLOCK, COLS), F32)] * 4,
        scratch_shapes=[
            pltpu.VMEM((4, PAIR, RANK), F32),
            pltpu.VMEM((4, PAIR, COLS), BF16),
            pltpu.VMEM((RANK, COLS), F32),
            pltpu.SemaphoreType.DMA((8, 2)),
        ],
        compiler_params=params(28),
        cost_estimate=SMALL,
        name="product",
    )(where, *[in_hbm(v) for v in power], in_hbm(lowered), *after)


def cross_kernel(where, p0, p1, p2, p3, x_ref, cross_low, cross, colsq, total):
    first = where[1]
    for step, piece in enumerate((p0, p1, p2, p3)):
        at = pl.multiple_of(lax.rem(first + step, 4) * BLOCK, BLOCK)
        total[pl.ds(at, BLOCK), :] = piece[...]
    half = RANK // 2
    value = jnp.concatenate(
        [dot3(x_ref[:half, :half], total[:half, :]), dot3(x_ref[half:, :], total[...])], axis=0
    )
    cross_low[...] = value.astype(BF16)
    turned = value.T
    cross[...] = turned
    colsq[...] = jnp.sum(turned * turned, axis=0, keepdims=True)


def cross_of(where, pieces, x):
    return pl.pallas_call(
        cross_kernel,
        grid_spec=pltpu.PrefetchScalarGridSpec(
            num_scalar_prefetch=1,
            grid=(1,),
            in_specs=[whole((BLOCK, COLS))] * 4 + [whole((RANK, RANK))],
            out_specs=[whole((RANK, COLS)), whole((COLS, RANK)), whole((1, RANK))],
            scratch_shapes=[pltpu.VMEM((RANK, COLS), F32)],
        ),
        out_shape=[
            jax.ShapeDtypeStruct((RANK, COLS), BF16),
            jax.ShapeDtypeStruct((COLS, RANK), F32),
            jax.ShapeDtypeStruct((1, RANK), F32),
        ],
        compiler_params=params(40),
        cost_estimate=SMALL,
        name="cross_of",
    )(where, *pieces, x)


def left_kernel(where, xt_high, xt_low, *refs):
    left, left_low, chunk = refs[-3:]
    for i in range(4):

        @pl.when(pl.program_id(0) == i)
        def _():
            for value, side in ((refs[2 * i], where[0]), (refs[2 * i + 1], 1 - where[0])):
                chunk[pl.ds(pl.multiple_of(side * CHUNK, 16), CHUNK), :] = value[...]

    high, low = halves(chunk[...])
    half = RANK // 2
    for rows, cols in ((half, slice(0, half)), (RANK, slice(half, RANK))):
        a, b = xt_high[:rows, cols], xt_low[:rows, cols]
        ortho = dot(high[:, :rows], a) + (dot(high[:, :rows], b) + dot(low[:, :rows], a))
        left[:, cols] = ortho * jnp.sqrt(F32(FF))
        left_low[:, cols] = ortho.astype(BF16)


def left_of(where, power, xt):
    tile = pl.BlockSpec((PAIR, RANK), lambda i, where: (lax.rem(where[3] + i, 4), 0))
    return pl.pallas_call(
        left_kernel,
        grid_spec=pltpu.PrefetchScalarGridSpec(
            num_scalar_prefetch=1,
            grid=(4,),
            in_specs=[VMEM] * 10,
            out_specs=[tile, tile],
            scratch_shapes=[pltpu.VMEM((PAIR, RANK), F32)],
        ),
        out_shape=[
            jax.ShapeDtypeStruct((ROWS, RANK), F32),
            jax.ShapeDtypeStruct((ROWS, RANK), BF16),
        ],
        compiler_params=params(16),
        cost_estimate=SMALL,
        name="left_of",
    )(where, *xt, *[in_vmem(value) for value in power])


def update_kernel(first, momentum, gradient, left_low, cross_low, *refs):
    feedback = dot(left_low[...], cross_low[...])
    at = (pl.program_id(0) + first) * CHUNK
    rows = pl.ds(pl.multiple_of(at, 32), CHUNK)
    refs[-1][...] = (momentum[rows] + gradient[rows].astype(F32)) - 0.05 * feedback


def update(first, momentum, gradient, left_low, cross_low, so_far=()):
    rows = lambda i: (i + first, 0)
    return pl.pallas_call(
        functools.partial(update_kernel, first),
        grid=(4,),
        in_specs=[VMEM, VMEM, pl.BlockSpec((CHUNK, RANK), rows), VMEM] + [ANY] * len(so_far),
        out_specs=pl.BlockSpec((CHUNK, COLS), rows),
        out_shape=jax.ShapeDtypeStruct((ROWS, COLS), F32),
        input_output_aliases={4: 0} if so_far else {},
        compiler_params=params(16),
        cost_estimate=SMALL,
        name="update",
    )(in_vmem(momentum), in_vmem(gradient), left_low, cross_low, *so_far)


def on_device(momentum, gradient, right_factor):
    row = lax.axis_index("row")
    col = lax.axis_index("col")
    x, z, y, core = row // 4, row % 4, col // 2, col % 2
    first = jnp.where(core == 0, x, z)
    second = jnp.where(core == 0, z, x)
    where = jnp.stack([core, first, second, y]).astype(jnp.int32)

    def chunks(side):
        return jnp.stack([2 * ((y + step) % 4) + side for step in ORDER]).astype(jnp.int32)

    asked = power_chunks(chunks(1 - core), momentum, gradient, right_factor, right_factor)
    received = [to_partner(value) for value in asked]
    kept = power_chunks(chunks(core), momentum, gradient, right_factor, asked[0])
    terms = {step: kept[i] + received[i] for i, step in enumerate(ORDER)}
    far = along_y(terms[2], 2)
    got = [far] + [tied(along_y(terms[step], step), far) for step in (1, 3)]
    lowered = lower(momentum, gradient, terms[3])
    own = total_of(terms[0], got, lowered)
    other = to_partner(own)
    own_all = gathered(own, along_y)

    gram = gram_part(core, own, other)
    gram_1 = exchanged_sum(gram, along_first, (own_all[1], own_all[3]))

    got = [along_second(gram_1, step) for step in (2, 1, 3)]
    mine = [own] + [tied(own_all[i], got if i == 2 else gram_1) for i in (1, 2, 3)]
    theirs = [other] + [to_partner(piece) for piece in mine[1:]]
    power = [half[step] for step in ORDER for half in (mine, theirs)]
    turned = product(where, power, lowered, [gram_1])

    gram_2 = total_of(gram_1, got, None)
    gram_3 = exchanged_sum(gram_2, along_y)
    turned = scattered_sum(turned, along_first, gram_3)
    state = inverse_first(where, tied(gram_3, turned), to_partner(gram_3))
    turned = exchanged_sum(turned, along_second, state[0])
    pieces = gathered(turned, along_first)

    inverse, *inverse_t = inverse_second(state, turned)
    power = [half[step] for step in range(4) for half in (mine, theirs)]
    left_factor, left_low = left_of(where, power, inverse_t)
    pieces = [tied(piece, left_low) for piece in pieces]
    cross_low, cross, colsq = cross_of(where, pieces, inverse)

    momentum_next = update(0, momentum, gradient, left_low, cross_low)
    colsq = exchanged_sum(colsq, along_y, momentum_next)
    colsq = colsq + to_partner(colsq)
    momentum_next = update(4, momentum, gradient, left_low, cross_low, (momentum_next,))
    colsq = tied(colsq, momentum_next)
    right_next = (cross / jnp.sqrt(colsq / D + 1e-06)).astype(BF16)
    return (left_factor, momentum_next, right_next)


def solution(mesh):
    in_specs = (P("row", "col"), P("row", "col"), P("col", None))
    out_specs = (P("row", None), P("row", "col"), P("col", None))
    return jax.shard_map(
        on_device, mesh=mesh, in_specs=in_specs, out_specs=out_specs, check_vma=False
    )
```

```python
import functools

import jax
import jax.numpy as jnp
from jax import lax
from jax.experimental import pallas as pl
from jax.experimental.pallas import tpu as pltpu
from jax.sharding import PartitionSpec as P

FF = 28672
D = 8192
RANK = 512
ROWS = 1792
COLS = 1024
CHUNK = 224
PAIR = 448
ORDER = (2, 1, 3, 0)
BLOCK = 128
AXES = ("row", "col")
HIGHEST = lax.Precision.HIGHEST
MIB = 2**20
F32 = jnp.float32
BF16 = jnp.bfloat16


def place(x, z, y, core):
    return (x * 4 + z) * 8 + y * 2 + core


def pairs_of(move):
    out = []
    for x in range(4):
        for z in range(4):
            for y in range(4):
                for core in range(2):
                    out.append((place(x, z, y, core), place(*move(x, z, y, core))))
    return out


def to_partner(value):
    return lax.ppermute(value, AXES, pairs_of(lambda x, z, y, core: (x, z, y, 1 - core)))


def along_y(value, step):
    return lax.ppermute(value, AXES, pairs_of(lambda x, z, y, core: (x, z, (y + step) % 4, core)))


def along_first(value, step):
    def move(x, z, y, core):
        return ((x + step) % 4, z, y, core) if core == 0 else (x, (z + step) % 4, y, core)

    return lax.ppermute(value, AXES, pairs_of(move))


def along_second(value, step):
    def move(x, z, y, core):
        return (x, (z + step) % 4, y, core) if core == 0 else ((x + step) % 4, z, y, core)

    return lax.ppermute(value, AXES, pairs_of(move))


def tied(value, after):
    return value if after is None else lax.optimization_barrier((value, after))[0]


def total_of(own, got, after):
    got = [tied(part, after) for part in got]
    return (own + got[0]) + (got[1] + got[2])


def scattered_sum(blocks, along, after=None):
    return total_of(blocks[0], [along(blocks[step], step) for step in (2, 1, 3)], after)


def exchanged_sum(value, along, after=None):
    return total_of(value, [along(value, step) for step in (2, 1, 3)], after)


def gathered(value, along):
    got = {step: along(value, -step) for step in (2, 1, 3)}
    return [value, got[1], got[2], got[3]]


def dot(a, b, precision=None):
    return lax.dot_general(
        a, b, (((1,), (0,)), ((), ())), precision=precision, preferred_element_type=F32
    )


def dot_t(a, b, precision=None):
    return lax.dot_general(
        a, b, (((0,), (0,)), ((), ())), precision=precision, preferred_element_type=F32
    )


def halves(value):
    high = value.astype(BF16)
    return high, (value - high.astype(F32)).astype(BF16)


def dot3(a, b):
    ah, al = halves(a)
    bh, bl = halves(b)
    return dot(ah, bh) + (dot(ah, bl) + dot(al, bh))


def params(mib):
    return pltpu.CompilerParams(vmem_limit_bytes=mib * MIB)


def in_vmem(value):
    return pltpu.with_memory_space_constraint(value, pltpu.VMEM)


def in_hbm(value):
    return pltpu.with_memory_space_constraint(value, pltpu.HBM)


VMEM = pl.BlockSpec(memory_space=pltpu.VMEM)
ANY = pl.BlockSpec(memory_space=pl.ANY)
SMEM = pl.BlockSpec(memory_space=pltpu.SMEM)


SMALL = pl.CostEstimate(flops=1, bytes_accessed=1, transcendentals=0)


LONG = pl.CostEstimate(flops=10**10, bytes_accessed=4 * MIB, transcendentals=0)


def chunk_at(where, first, i):
    side = jnp.where(lax.rem(i, 2) == 0, where[0], 1 - where[0])
    return 2 * lax.rem(where[3] + first + i // 2, 4) + side


def whole(shape):
    return pl.BlockSpec(shape, lambda *_: (0,) * len(shape))


def power_kernel(n, where, momentum, gradient, right, after, *refs):
    power = refs[:n]
    m, g, q, sems, q_sem = refs[n:]
    copies = []
    for i in range(n):
        source = pl.ds(pl.multiple_of(where[i] * CHUNK, 16), CHUNK)
        for j, (array, slots) in enumerate(((momentum, m), (gradient, g))):
            copy = pltpu.make_async_copy(array.at[source], slots.at[i], sems.at[i, j])
            copy.start()
            copies.append(copy)
        if i == 0:
            q_copy = pltpu.make_async_copy(right, q, q_sem)
            q_copy.start()
    for i in range(n):
        copies[2 * i].wait()
        copies[2 * i + 1].wait()
        if i == 0:
            q_copy.wait()
        power[i][...] = dot((m[i] + g[i].astype(F32)).astype(BF16), q[...])


def power_chunks(where, momentum, gradient, right, after):
    n = where.shape[0]
    return pl.pallas_call(
        functools.partial(power_kernel, n),
        in_specs=[SMEM] + [ANY] * 4,
        out_specs=[VMEM] * n,
        out_shape=[jax.ShapeDtypeStruct((CHUNK, RANK), F32)] * n,
        scratch_shapes=[
            pltpu.VMEM((n, CHUNK, COLS), F32),
            pltpu.VMEM((n, CHUNK, COLS), BF16),
            pltpu.VMEM((COLS, RANK), BF16),
            pltpu.SemaphoreType.DMA((n, 2)),
            pltpu.SemaphoreType.DMA,
        ],
        compiler_params=params(24),
        cost_estimate=SMALL,
        name="power_chunks",
    )(where, in_hbm(momentum), in_hbm(gradient), in_hbm(right), after)


def lower_kernel(momentum, gradient, after, lowered):
    lowered[...] = (momentum[...] + gradient[...].astype(F32)).astype(BF16)


def lower(momentum, gradient, after):
    tile = pl.BlockSpec((CHUNK, COLS), lambda i: (i, 0))
    return pl.pallas_call(
        lower_kernel,
        grid=(8,),
        in_specs=[tile, tile, ANY],
        out_specs=tile,
        out_shape=pltpu.HBM((ROWS, COLS), BF16),
        compiler_params=params(16),
        cost_estimate=SMALL,
        name="lower",
    )(in_hbm(momentum), in_hbm(gradient), after)


def gram_kernel(where, own, other, out):
    def strip(lo, hi, at):
        total = dot_t(own[:, lo:hi], own[:, at : at + BLOCK], HIGHEST)
        return total + dot_t(other[:, lo:hi], other[:, at : at + BLOCK], HIGHEST)

    @pl.when(where[0] == 0)
    def _():
        out[0:128] = strip(0, 128, 0)
        out[128:640] = strip(0, 512, 384)

    @pl.when(where[0] == 1)
    def _():
        out[0:256] = strip(0, 256, 128)
        out[256:640] = strip(0, 384, 256)


def gram_part(core, own, other):
    return pl.pallas_call(
        gram_kernel,
        grid_spec=pltpu.PrefetchScalarGridSpec(
            num_scalar_prefetch=1,
            grid=(1,),
            in_specs=[whole((CHUNK, RANK))] * 2,
            out_specs=whole((640, BLOCK)),
        ),
        out_shape=jax.ShapeDtypeStruct((640, BLOCK), F32),
        compiler_params=params(16),
        cost_estimate=SMALL,
        name="gram_part",
    )(core.reshape(1), own, other)


def block_inverse(matrix, beside=()):
    beside = list(beside)
    tile = (8, BLOCK)
    rows = lax.broadcasted_iota(jnp.int32, tile, 0)
    lanes = lax.broadcasted_iota(jnp.int32, tile, 1)
    W = [matrix[8 * g : 8 * g + 8, :] for g in range(16)]
    out = []

    def columns(value, at):
        return [jnp.broadcast_to(value[:, at + k : at + k + 1], tile) for k in range(8)]

    for p in range(16):
        at = 8 * p
        col = columns(W[p], at)
        one = {(k, l): jnp.broadcast_to(col[k][l : l + 1, :], tile) for k in range(8) for l in range(k, 8)}
        panel = (lanes >= at) & (lanes < at + 8)
        own = jnp.where(panel, (lanes - at == rows).astype(F32), W[p])
        row = [jnp.broadcast_to(own[k : k + 1, :], tile) for k in range(8)]
        done, steps = [], []
        for k in range(0, 8, 2):
            a, b, d = one[k, k], one[k, k + 1], one[k + 1, k + 1]
            det = a * d - b * b
            inv = 1.0 / det
            u, v = {}, {}
            for l in range(k + 2, 8):
                u[l] = (d * one[k, l] - b * one[k + 1, l]) * inv
                v[l] = (a * one[k + 1, l] - b * one[k, l]) * inv
            for i in range(k + 2, 8):
                for l in range(i, 8):
                    one[i, l] = one[i, l] - (one[k, i] * u[l] + one[k + 1, i] * v[l])
            r, s = row[k], row[k + 1]
            for l in range(k + 2, 8):
                row[l] = row[l] - (r * u[l] + s * v[l])
            steps.append((k, u, v, (d * r - b * s) * inv, (a * s - b * r) * inv))
            inv_a = 1.0 / a
            done.append(r * lax.rsqrt(a))
            done.append((s - r * (b * inv_a)) * lax.rsqrt(det * inv_a))
        result = done[0]
        for k in range(1, 8):
            result = jnp.where(rows == k, done[k], result)
        out.append(jnp.where(lanes < at + 8, result, 0.0))
        for g in range(p + 1, 16):
            col = columns(W[g], at)
            total = None
            for k, u, v, first, second in steps:
                term = col[k] * first + col[k + 1] * second
                total = term if total is None else total + term
                for l in range(k + 2, 8):
                    col[l] = col[l] - (col[k] * u[l] + col[k + 1] * v[l])
            W[g] = jnp.where(panel, 0.0, W[g]) - total
        if beside and p % 2 == 1:
            beside.pop(0)()
    for step in beside:
        step()
    return jnp.concatenate(out, axis=0)


def eliminate(x_ref, a, e, starts):
    for lo in starts:
        hi, before = lo + BLOCK, lo - BLOCK
        diagonal = a[lo:hi, lo:hi]
        beside = []
        if lo > 0:
            last = x_ref[before:lo, before:lo]
            upper = {lo: dot(last, a[before:lo, lo:hi], HIGHEST)}
            diagonal = diagonal - dot_t(upper[lo], upper[lo], HIGHEST)

            def strip(at):
                def step():
                    upper[at] = dot(last, a[before:lo, at : at + BLOCK], HIGHEST)
                    for row in range(lo, at + BLOCK, BLOCK):
                        block = (slice(row, row + BLOCK), slice(at, at + BLOCK))
                        a[block] = a[block] - dot_t(upper[row], upper[at], HIGHEST)

                return step

            def rows_of_e(at):
                def step():
                    block = (slice(at, at + BLOCK), slice(0, lo))
                    e[block] = e[block] - dot_t(upper[at], x_ref[before:lo, :lo], HIGHEST)

                return step

            beside = [rows_of_e(lo)]
            for at in range(hi, RANK, BLOCK):
                beside += [strip(at), rows_of_e(at)]
        inverse = block_inverse(diagonal, beside)
        x_ref[lo:hi, lo:hi] = inverse
        if lo > 0:
            x_ref[lo:hi, :lo] = dot(inverse, e[lo:hi, :lo], HIGHEST)


def first_kernel(where, mine, theirs, x_ref, a, e, strips):
    strips[where[0]] = mine[...]
    strips[1 - where[0]] = theirs[...]
    a[0:128, 0:128] = strips[0, 0:128]
    a[0:512, 384:512] = strips[0, 128:640]
    a[0:256, 128:256] = strips[1, 0:256]
    a[0:384, 256:384] = strips[1, 256:640]
    x_ref[...] = jnp.zeros_like(x_ref)
    e[...] = jnp.zeros_like(e)
    eliminate(x_ref, a, e, (0, 128, 256))


def second_kernel(x_in, a_in, e_in, after, x_ref, high, low, a, e):
    x_ref[...] = x_in[...]
    a[256:, 384:] = a_in[256:, 384:]
    e[384:, :] = e_in[384:, :]
    eliminate(x_ref, a, e, (384,))
    high[...], low[...] = halves(x_ref[...].T)


def inverse_first(where, mine, theirs):
    square = jax.ShapeDtypeStruct((RANK, RANK), F32)
    return pl.pallas_call(
        first_kernel,
        grid_spec=pltpu.PrefetchScalarGridSpec(
            num_scalar_prefetch=1,
            grid=(1,),
            in_specs=[whole((640, BLOCK))] * 2,
            out_specs=[whole((RANK, RANK))] * 3,
            scratch_shapes=[pltpu.VMEM((2, 640, BLOCK), F32)],
        ),
        out_shape=[square] * 3,
        compiler_params=params(24),
        cost_estimate=LONG,
        name="inverse_first",
    )(where, mine, theirs)


def inverse_second(state, after):
    square = jax.ShapeDtypeStruct((RANK, RANK), F32)
    return pl.pallas_call(
        second_kernel,
        grid=(1,),
        in_specs=[whole((RANK, RANK))] * 3 + [pl.BlockSpec(memory_space=pl.ANY)],
        out_specs=[whole((RANK, RANK))] * 3,
        out_shape=[square] + [jax.ShapeDtypeStruct((RANK, RANK), BF16)] * 2,
        scratch_shapes=[pltpu.VMEM((RANK, RANK), F32)] * 2,
        compiler_params=params(24),
        cost_estimate=LONG,
        name="inverse_second",
    )(*state, after)


def ordered(chunk, rows, core, own, other):
    for value, side in ((own, core), (other, 1 - core)):
        chunk[pl.ds(pl.multiple_of(rows + side * CHUNK, 16), CHUNK), :] = value


def product_kernel(where, *refs):
    power_in, lowered = refs[0:8], refs[8]
    out = refs[-8:-4]
    power, low, total, sems = refs[-4:]
    copies = []
    for i in range(8):
        rows = pl.ds((i % 2) * CHUNK, CHUNK)
        at = pl.multiple_of(chunk_at(where, 0, 2 * ORDER[i // 2] + i % 2) * CHUNK, 16)
        source = lowered.at[pl.ds(at, CHUNK)]
        for j, (source, target) in enumerate(((power_in[i], power), (source, low))):
            copy = pltpu.make_async_copy(source, target.at[i // 2, rows], sems.at[i, j])
            copy.start()
            copies.append(copy)
    for i in range(4):
        for copy in copies[4 * i : 4 * i + 4]:
            copy.wait()
        first, second = halves(power[i])
        for at in range(0, COLS, 256):
            tall = low[i, :, at : at + 256]
            value = dot_t(second, tall) + dot_t(first, tall)
            if i > 0:
                value = value + total[:, at : at + 256]
            total[:, at : at + 256] = value
    for step in range(4):
        rows = pl.multiple_of(lax.rem(where[1] + step, 4) * BLOCK, BLOCK)
        out[step][...] = total[pl.ds(rows, BLOCK), :]


def product(where, power, lowered, after):
    return pl.pallas_call(
        product_kernel,
        in_specs=[SMEM] + [ANY] * (9 + len(after)),
        out_specs=[VMEM] * 4,
        out_shape=[jax.ShapeDtypeStruct((BLOCK, COLS), F32)] * 4,
        scratch_shapes=[
            pltpu.VMEM((4, PAIR, RANK), F32),
            pltpu.VMEM((4, PAIR, COLS), BF16),
            pltpu.VMEM((RANK, COLS), F32),
            pltpu.SemaphoreType.DMA((8, 2)),
        ],
        compiler_params=params(28),
        cost_estimate=SMALL,
        name="product",
    )(where, *[in_hbm(v) for v in power], in_hbm(lowered), *after)


def cross_kernel(where, p0, p1, p2, p3, x_ref, cross_low, cross, colsq, total):
    first = where[1]
    for step, piece in enumerate((p0, p1, p2, p3)):
        at = pl.multiple_of(lax.rem(first + step, 4) * BLOCK, BLOCK)
        total[pl.ds(at, BLOCK), :] = piece[...]
    half = RANK // 2
    value = jnp.concatenate(
        [dot3(x_ref[:half, :half], total[:half, :]), dot3(x_ref[half:, :], total[...])], axis=0
    )
    cross_low[...] = value.astype(BF16)
    turned = value.T
    cross[...] = turned
    colsq[...] = jnp.sum(turned * turned, axis=0, keepdims=True)


def cross_of(where, pieces, x):
    return pl.pallas_call(
        cross_kernel,
        grid_spec=pltpu.PrefetchScalarGridSpec(
            num_scalar_prefetch=1,
            grid=(1,),
            in_specs=[whole((BLOCK, COLS))] * 4 + [whole((RANK, RANK))],
            out_specs=[whole((RANK, COLS)), whole((COLS, RANK)), whole((1, RANK))],
            scratch_shapes=[pltpu.VMEM((RANK, COLS), F32)],
        ),
        out_shape=[
            jax.ShapeDtypeStruct((RANK, COLS), BF16),
            jax.ShapeDtypeStruct((COLS, RANK), F32),
            jax.ShapeDtypeStruct((1, RANK), F32),
        ],
        compiler_params=params(40),
        cost_estimate=SMALL,
        name="cross_of",
    )(where, *pieces, x)


def left_kernel(where, xt_high, xt_low, *refs):
    left, left_low, chunk = refs[-3:]
    for i in range(4):

        @pl.when(pl.program_id(0) == i)
        def _():
            for value, side in ((refs[2 * i], where[0]), (refs[2 * i + 1], 1 - where[0])):
                chunk[pl.ds(pl.multiple_of(side * CHUNK, 16), CHUNK), :] = value[...]

    high, low = halves(chunk[...])
    half = RANK // 2
    for rows, cols in ((half, slice(0, half)), (RANK, slice(half, RANK))):
        a, b = xt_high[:rows, cols], xt_low[:rows, cols]
        ortho = dot(high[:, :rows], a) + (dot(high[:, :rows], b) + dot(low[:, :rows], a))
        left[:, cols] = ortho * jnp.sqrt(F32(FF))
        left_low[:, cols] = ortho.astype(BF16)


def left_of(where, power, xt):
    tile = pl.BlockSpec((PAIR, RANK), lambda i, where: (lax.rem(where[3] + i, 4), 0))
    return pl.pallas_call(
        left_kernel,
        grid_spec=pltpu.PrefetchScalarGridSpec(
            num_scalar_prefetch=1,
            grid=(4,),
            in_specs=[VMEM] * 10,
            out_specs=[tile, tile],
            scratch_shapes=[pltpu.VMEM((PAIR, RANK), F32)],
        ),
        out_shape=[
            jax.ShapeDtypeStruct((ROWS, RANK), F32),
            jax.ShapeDtypeStruct((ROWS, RANK), BF16),
        ],
        compiler_params=params(16),
        cost_estimate=SMALL,
        name="left_of",
    )(where, *xt, *[in_vmem(value) for value in power])


def update_kernel(first, momentum, gradient, left_low, cross_low, *refs):
    feedback = dot(left_low[...], cross_low[...])
    at = (pl.program_id(0) + first) * CHUNK
    rows = pl.ds(pl.multiple_of(at, 32), CHUNK)
    refs[-1][...] = (momentum[rows] + gradient[rows].astype(F32)) - 0.05 * feedback


def update(first, momentum, gradient, left_low, cross_low, so_far=()):
    rows = lambda i: (i + first, 0)
    return pl.pallas_call(
        functools.partial(update_kernel, first),
        grid=(4,),
        in_specs=[VMEM, VMEM, pl.BlockSpec((CHUNK, RANK), rows), VMEM] + [ANY] * len(so_far),
        out_specs=pl.BlockSpec((CHUNK, COLS), rows),
        out_shape=jax.ShapeDtypeStruct((ROWS, COLS), F32),
        input_output_aliases={4: 0} if so_far else {},
        compiler_params=params(16),
        cost_estimate=SMALL,
        name="update",
    )(in_vmem(momentum), in_vmem(gradient), left_low, cross_low, *so_far)


def on_device(momentum, gradient, right_factor):
    row = lax.axis_index("row")
    col = lax.axis_index("col")
    x, z, y, core = row // 4, row % 4, col // 2, col % 2
    first = jnp.where(core == 0, x, z)
    second = jnp.where(core == 0, z, x)
    where = jnp.stack([core, first, second, y]).astype(jnp.int32)

    def chunks(side):
        return jnp.stack([2 * ((y + step) % 4) + side for step in ORDER]).astype(jnp.int32)

    asked = power_chunks(chunks(1 - core), momentum, gradient, right_factor, right_factor)
    received = [to_partner(value) for value in asked]
    kept = power_chunks(chunks(core)[:1], momentum, gradient, right_factor, asked[0])
    terms = {2: kept[0] + received[0]}
    kept = power_chunks(chunks(core)[1:], momentum, gradient, right_factor, terms[2])
    for i, step in enumerate(ORDER[1:]):
        terms[step] = kept[i] + received[i + 1]
    far = along_y(terms[2], 2)
    got = [far] + [tied(along_y(terms[step], step), far) for step in (1, 3)]
    lowered = lower(momentum, gradient, terms[3])
    own = total_of(terms[0], got, lowered)
    other = to_partner(own)
    own_all = gathered(own, along_y)

    gram = gram_part(core, own, other)
    gram_1 = exchanged_sum(gram, along_first, (own_all[1], own_all[3]))

    got = [along_second(gram_1, step) for step in (2, 1, 3)]
    mine = [own] + [tied(own_all[i], got if i == 2 else gram_1) for i in (1, 2, 3)]
    theirs = [other] + [to_partner(piece) for piece in mine[1:]]
    power = [half[step] for step in ORDER for half in (mine, theirs)]
    turned = product(where, power, lowered, [gram_1])

    gram_2 = total_of(gram_1, got, None)
    gram_3 = exchanged_sum(gram_2, along_y)
    turned = scattered_sum(turned, along_first, gram_3)
    state = inverse_first(where, tied(gram_3, turned), to_partner(gram_3))
    turned = exchanged_sum(turned, along_second, state[0])
    pieces = gathered(turned, along_first)

    inverse, *inverse_t = inverse_second(state, turned)
    power = [half[step] for step in range(4) for half in (mine, theirs)]
    left_factor, left_low = left_of(where, power, inverse_t)
    pieces = [tied(piece, left_low) for piece in pieces]
    cross_low, cross, colsq = cross_of(where, pieces, inverse)

    momentum_next = update(0, momentum, gradient, left_low, cross_low)
    colsq = exchanged_sum(colsq, along_y, momentum_next)
    colsq = colsq + to_partner(colsq)
    momentum_next = update(4, momentum, gradient, left_low, cross_low, (momentum_next,))
    colsq = tied(colsq, momentum_next)
    right_next = (cross / jnp.sqrt(colsq / D + 1e-06)).astype(BF16)
    return (left_factor, momentum_next, right_next)


def solution(mesh):
    in_specs = (P("row", "col"), P("row", "col"), P("col", None))
    out_specs = (P("row", None), P("row", "col"), P("col", None))
    return jax.shard_map(
        on_device, mesh=mesh, in_specs=in_specs, out_specs=out_specs, check_vma=False
    )
```
